128 devices in a mesh: wa: 32 (over x, y, core), vert: 4 (over z).
Axes of the slice: x: 4, y: 4, z: 4, core: 2. Of those that a mesh axis runs over, the one named last changes fastest.
Arguments:
- grid_values: bfloat16 [1024, 64, 5376], P('wa', 'vert'), may hold values from -6 to 6
- row_length: int32 [1024], P('wa'), may hold values from 20 to 5136, as said below
- pair_order: int32 [640], replicated, may hold values from 0 to 639, each once
- legendre: bfloat16 [640, 512, 1281], P(('wa', 'vert')), may hold values from -0.25 to 0.25
Outputs:
- spectral: float32 [640, 2, 64, 1281], P(('wa', 'vert'))
The draws below stay inside these ranges and needn't reach their ends.
Inputs may be any that keep to these rules, and one draw needn't show every extreme that they name: `row_length`: row r and row 512 + r have the same length; the first 512 lengths are 20 + 4 j for distinct j, strictly increasing, and the last of them is 5136. `pair_order`: every pair stands in exactly one slot.
All inputs are finite; a program needn't handle non-finite values.
Results may differ from the reference program's by a relative error of at most 0.0048.
Values may be sent and summed in bfloat16 or wider, within the bound.
A program may use at most 128 MiB of HBM per device.

```python
import math
import jax
import jax.numpy as jnp
from jax import lax

TRUNC = 1279
SUB = 256
LPAD = 5376
PAIRS = 640
NCOL = 1281
ROWS = 1024
NLAT = 512
FIELDS = 64


def draw_row_length(key, part):
    shuffled = jax.random.permutation(key, TRUNC)
    chosen = jnp.sort(shuffled[:NLAT - 1].astype(jnp.int32))
    latitudes = jnp.concatenate([chosen, jnp.full((1,), TRUNC, jnp.int32)])
    lengths = 20 + 4 * latitudes
    return jnp.concatenate([lengths, lengths]).astype(jnp.int32)


def shard_levels(rng, shape, cuts, least, largest):
    loudness = 1.0
    for dim, shards_of in cuts:
        heights = jax.random.uniform(jax.random.fold_in(jax.random.fold_in(rng, 6), dim), (shards_of,), jnp.float32, least / len(cuts), largest / len(cuts))
        loudness = loudness * jnp.repeat(jnp.exp(heights), shape[dim] // shards_of).reshape((-1,) + (1,) * (len(shape) - 1 - dim))
    return loudness


def noise(stream_key, shape, spread, limit, shards=(), held_as=jnp.bfloat16):
    loudness = shard_levels(stream_key, shape, shards, -0.22, 0.18) if shards else 1.0
    entries = jax.random.normal(stream_key, shape, jnp.float32) * spread * loudness
    return jnp.minimum(jnp.maximum(entries, -limit), limit).astype(held_as)


def setup_inputs(seed: int = 0) -> dict:
    keys = jax.random.split(jax.random.key(seed), 5)
    return {
        "grid_values": noise(keys[0], (ROWS, FIELDS, LPAD), 1.0, 6.0, ((0, 32), (1, 4))),
        "row_length": draw_row_length(jax.random.fold_in(keys[4], 71), 0),
        "pair_order": jax.random.permutation(keys[2], PAIRS).astype(jnp.int32),
        "legendre": noise(keys[3], (PAIRS, NLAT, NCOL), NLAT ** -0.5, 0.25, ((0, 128),)),
    }


def row_tables(length):
    wave_ids = jnp.arange(TRUNC + 1, dtype=jnp.int32)
    points = jnp.arange(SUB, dtype=jnp.int32)
    blocks = jnp.arange(LPAD // SUB, dtype=jnp.int32)
    length_float = length.astype(jnp.float32)
    step_angle = 2.0 * math.pi / length_float
    inner_angle = (points[:, None] * wave_ids[None, :] % length).astype(jnp.float32) * step_angle
    inner_table = jnp.concatenate([jnp.cos(inner_angle), -jnp.sin(inner_angle)], axis=1).astype(jnp.bfloat16)
    outer_angle = (blocks[:, None] * (SUB * wave_ids)[None, :] % length).astype(jnp.float32) * step_angle
    keep_scale = (wave_ids <= (length - 1) // 2).astype(jnp.float32) / jnp.sqrt(length_float)
    return (inner_table, jnp.cos(outer_angle), -jnp.sin(outer_angle), keep_scale)

def fourier_row(grid_row, length):
    inner_table, twist_cos, twist_sin, keep_scale = row_tables(length)
    field_count = grid_row.shape[0]
    block_total = LPAD // SUB
    wave_total = TRUNC + 1
    valid = jnp.arange(LPAD, dtype=jnp.int32) < length
    masked = jnp.where(valid[None, :], grid_row, jnp.zeros_like(grid_row))
    partial_value = jnp.dot(masked.reshape(field_count * block_total, SUB).astype(jnp.float32), inner_table.astype(jnp.float32), precision=lax.Precision.HIGHEST, preferred_element_type=jnp.float32)
    partial_value = partial_value.reshape(field_count, block_total, 2 * wave_total)
    cos_part = partial_value[:, :, :wave_total]
    sin_part = partial_value[:, :, wave_total:]
    real_part = lax.optimization_barrier(jnp.sum(cos_part * twist_cos - sin_part * twist_sin, axis=1)) * keep_scale
    imag_part = lax.optimization_barrier(jnp.sum(cos_part * twist_sin + sin_part * twist_cos, axis=1)) * keep_scale
    return jnp.stack([real_part, imag_part], axis=1).astype(jnp.bfloat16)

def reference(grid_values, row_length, pair_order, legendre):
    fourier = lax.map(lambda row_item: fourier_row(row_item[0], row_item[1]), (grid_values, row_length))
    north_rows = fourier[:NLAT].astype(jnp.float32)
    south_rows = fourier[NLAT:].astype(jnp.float32)
    sym_part = (north_rows + south_rows).astype(jnp.bfloat16)
    anti_part = (north_rows - south_rows).astype(jnp.bfloat16)

    def one_slot(slot_item):
        leg_table, pair_id = slot_item
        col_ids = jnp.stack([pair_id, TRUNC - pair_id]).astype(jnp.int32)
        sym_cols = jnp.take(sym_part, col_ids, axis=3)
        anti_cols = jnp.take(anti_part, col_ids, axis=3)
        stacked = jnp.stack([sym_cols, anti_cols], axis=0)
        operand = jnp.transpose(stacked, (1, 4, 0, 3, 2)).reshape(NLAT, 8 * FIELDS)
        product = jnp.dot(leg_table.astype(jnp.float32).T, operand.astype(jnp.float32), precision=lax.Precision.HIGHEST, preferred_element_type=jnp.float32)
        product = product.reshape(NCOL, 4, 2, FIELDS)
        column = jnp.arange(NCOL, dtype=jnp.int32)
        first_count = TRUNC + 1 - pair_id
        in_first = column < first_count
        degree = jnp.where(in_first, column, column - first_count)
        group_idx = jnp.where(in_first, 0, 2) + degree % 2
        pick_mask = (group_idx[:, None] == jnp.arange(4, dtype=jnp.int32)[None, :]).astype(jnp.float32)
        chosen = lax.optimization_barrier(jnp.sum(product * pick_mask[:, :, None, None], axis=1))
        return jnp.transpose(chosen, (1, 2, 0))
    return lax.map(one_slot, (legendre, pair_order))
```

```python
import functools
import math

import jax
import jax.numpy as jnp
from jax import lax
from jax.experimental import pallas as pl
from jax.experimental.pallas import tpu as pltpu
from jax.sharding import PartitionSpec as P

TRUNC = 1279
SUB = 256
LPAD = 5376
WAVES = TRUNC + 1
CLASS = WAVES // 4
CPAD = 384
LANE = 128
CHUNKS = 11
BLOCKS = 6
GROUPS = 8
SPAN = 4


def sincos(turns):
    quarter = turns * 4.0
    near = jnp.floor(quarter + 0.5)
    f = quarter - near
    f2 = f * f
    h = math.pi / 2
    s = f * (h + f2 * (-(h**3) / 6 + f2 * (h**5 / 120 + f2 * (-(h**7) / 5040 + f2 * (h**9 / 362880)))))
    c = 1.0 + f2 * (
        -(h**2) / 2 + f2 * (h**4 / 24 + f2 * (-(h**6) / 720 + f2 * (h**8 / 40320 - f2 * (h**10 / 3628800))))
    )
    which = near - 4.0 * jnp.floor(near * 0.25)
    odd = (which == 1.0) | (which == 3.0)
    cos_out = jnp.where(odd, s, c)
    sin_out = jnp.where(odd, c, s)
    cos_out = jnp.where((which == 1.0) | (which == 2.0), -cos_out, cos_out)
    sin_out = jnp.where(which >= 2.0, -sin_out, sin_out)
    return cos_out, sin_out


def turns_of(product, n_float, inv_n):
    return (product - jnp.floor(product * inv_n) * n_float) * inv_n


def iota_f(shape, dim):
    return lax.broadcasted_iota(jnp.int32, shape, dim).astype(jnp.float32)


def fourier_kernel(quarter_ref, inv_ref, scale_ref, grid_ref, order_ref, out_ref, lhs, rhs, tens, onehot, rows, spread):
    g = pl.program_id(0)

    @pl.when(g == 0)
    def _():
        lhs[...] = jnp.zeros_like(lhs)
        for r in range(4):
            wave = lax.broadcasted_iota(jnp.int32, (WAVES, CPAD), 1) * 4 + r
            wave = jnp.where(wave < WAVES, wave, -1)
            onehot[:, r * CPAD : (r + 1) * CPAD] = (wave == order_ref[...]).astype(jnp.float32).astype(jnp.bfloat16)

    def one_row(t, carry):
        row = t * GROUPS + g
        n = quarter_ref[row]
        inv_n = inv_ref[row]
        scale = scale_ref[row]
        n_float = n.astype(jnp.float32)

        u = iota_f((8, CPAD), 1)
        low = iota_f((8, CPAD), 0)
        base = []
        for half in range(2):
            c, s = sincos(turns_of((low + 8.0 * half) * u, n_float, inv_n))
            base.append((c, s))
            c, s = sincos(turns_of((low + 8.0 * half) * 16.0 * u, n_float, inv_n))
            tens[0, half * 8 : half * 8 + 8] = c
            tens[1, half * 8 : half * 8 + 8] = s
        for a in range(16):
            ca = tens[0, a : a + 1, :]
            sa = tens[1, a : a + 1, :]
            c = jnp.concatenate([cb * ca - sb * sa for cb, sb in base], axis=0)
            s = jnp.concatenate([sb * ca + cb * sa for cb, sb in base], axis=0)
            c16 = c.astype(jnp.bfloat16)
            s16 = s.astype(jnp.bfloat16)
            rhs[a * 16 : a * 16 + 16, :CPAD] = c16
            rhs[a * 16 : a * 16 + 16, CPAD:] = (-s).astype(jnp.bfloat16)
            rhs[SUB + a * 16 : SUB + a * 16 + 16, :CPAD] = s16
            rhs[SUB + a * 16 : SUB + a * 16 + 16, CPAD:] = c16

        lane = lax.broadcasted_iota(jnp.int32, (16, LANE), 1)
        quarters = []
        for part in range(4):
            start = n * part
            whole = start // LANE
            shift = start - whole * LANE
            count = CHUNKS + (1 if part else 0)
            pieces = [
                grid_ref[t, 0, :, pl.ds(pl.multiple_of((whole + j) * LANE, LANE), LANE)].astype(jnp.float32)
                for j in range(count)
            ]
            if part:
                back = lax.rem(LANE - shift, LANE)
                turned = [pltpu.roll(piece, back, 1) for piece in pieces]
                keep = lane < LANE - shift
                pieces = [jnp.where(keep, turned[j], turned[j + 1]) for j in range(CHUNKS)]
            quarters.append(pieces)

        lane8 = lax.broadcasted_iota(jnp.int32, (8, LANE), 1)
        for j in range(CHUNKS):
            k = lane8 + j * LANE
            inside = k < n
            c1, s1 = sincos(k.astype(jnp.float32) * (inv_n * 0.25))
            c2 = c1 * c1 - s1 * s1
            s2 = 2.0 * c1 * s1
            c3 = c2 * c1 - s2 * s1
            s3 = s2 * c1 + c2 * s1

            def both(v):
                v = jnp.where(inside, v, 0.0)
                return jnp.concatenate([v, v], axis=0)

            c1, s1, c2, s2, c3, s3 = (both(v) for v in (c1, s1, c2, s2, c3, s3))
            qa, qb, qc, qd = (quarters[part][j] for part in range(4))
            even = qa + qc
            even_other = qb + qd
            re = qa - qc
            im = qd - qb
            h0 = jnp.where(lane + j * LANE < n, even + even_other, 0.0)
            h2 = even - even_other
            values = (
                (h0, None),
                (re * c1 + im * s1, im * c1 - re * s1),
                (h2 * c2, -(h2 * s2)),
                (re * c3 - im * s3, -(im * c3 + re * s3)),
            )
            q = j // 2
            at = (j % 2) * LANE
            for r, (zr, zi) in enumerate(values):
                top = (r * BLOCKS + q) * 16
                lhs[top : top + 16, at : at + LANE] = zr.astype(jnp.bfloat16)
                if zi is not None:
                    lhs[top : top + 16, SUB + at : SUB + at + LANE] = zi.astype(jnp.bfloat16)

        part_sum = jnp.dot(lhs[...], rhs[...], preferred_element_type=jnp.float32)

        tc, ts = sincos(turns_of(low * 256.0 * u, n_float, inv_n))
        column = lax.broadcasted_iota(jnp.int32, (1, CPAD), 1)
        lane_top = pl.multiple_of((g % 2) * LANE + t * 32, 32)
        for r in range(4):
            real = part_sum[r * 96 : r * 96 + 16, :CPAD]
            imag = part_sum[r * 96 : r * 96 + 16, CPAD:]
            for q in range(1, BLOCKS):
                top = r * 96 + q * 16
                pr = part_sum[top : top + 16, :CPAD]
                pi = part_sum[top : top + 16, CPAD:]
                c = tc[q : q + 1, :]
                s = ts[q : q + 1, :]
                real = real + (pr * c + pi * s)
                imag = imag + (pi * c - pr * s)
            wave = column * 4 + r
            keep = jnp.where((wave <= 2 * n - 1) & (column < CLASS), scale, 0.0)
            rows[pl.ds(lane_top, 16), r * CPAD : (r + 1) * CPAD] = (real * keep).astype(jnp.bfloat16)
            rows[pl.ds(lane_top + 16, 16), r * CPAD : (r + 1) * CPAD] = (imag * keep).astype(jnp.bfloat16)
        return carry

    lax.fori_loop(0, SPAN, one_row, 0)

    @pl.when(g % 2 == 1)
    def _():
        step = 256

        def order(i, carry):
            top = pl.multiple_of(i * step, step)
            picked = lax.dot_general(
                onehot[pl.ds(top, step), :],
                rows[...],
                (((1,), (1,)), ((), ())),
                preferred_element_type=jnp.float32,
            )
            spread[pl.ds(top * GROUPS + g - 1, step, stride=GROUPS), :] = picked[:, :LANE]
            spread[pl.ds(top * GROUPS + g, step, stride=GROUPS), :] = picked[:, LANE:]
            return carry

        lax.fori_loop(0, WAVES // step, order, 0)

    @pl.when(g == GROUPS - 1)
    def _():
        dest_rows = out_ref.shape[1]

        def finish(d, carry):
            out_ref[d] = spread[pl.ds(pl.multiple_of(d * dest_rows, dest_rows), dest_rows), :].astype(jnp.bfloat16)
            return carry

        lax.fori_loop(0, out_ref.shape[0], finish, 0)


def fourier_all(grid_values, row_length, order, device_total):
    row_total, field_count, points = grid_values.shape
    quarter = row_length // 4
    length_float = row_length.astype(jnp.float32)
    inv_n = 1.0 / quarter.astype(jnp.float32)
    scale = 1.0 / jnp.sqrt(length_float)
    smem = pl.BlockSpec(memory_space=pltpu.SMEM)
    dest_rows = WAVES * GROUPS // device_total
    return pl.pallas_call(
        fourier_kernel,
        grid=(GROUPS,),
        in_specs=[
            smem,
            smem,
            smem,
            pl.BlockSpec((SPAN, 1, field_count, points), lambda g: (0, g, 0, 0)),
            pl.BlockSpec((WAVES, 1), lambda g: (0, 0)),
        ],
        out_specs=pl.BlockSpec((device_total, dest_rows, LANE), lambda g: (0, 0, 0)),
        out_shape=jax.ShapeDtypeStruct((device_total, dest_rows, LANE), jnp.bfloat16),
        scratch_shapes=[
            pltpu.VMEM((4 * BLOCKS * 16, 2 * SUB), jnp.bfloat16),
            pltpu.VMEM((2 * SUB, 2 * CPAD), jnp.bfloat16),
            pltpu.VMEM((2, 16, CPAD), jnp.float32),
            pltpu.VMEM((WAVES, 4 * CPAD), jnp.bfloat16),
            pltpu.VMEM((2 * LANE, 4 * CPAD), jnp.bfloat16),
            pltpu.VMEM((WAVES * GROUPS, LANE), jnp.float32),
        ],
        compiler_params=pltpu.CompilerParams(vmem_limit_bytes=48 * 2**20),
        name="fourier",
    )(quarter, inv_n, scale, grid_values.reshape(SPAN, GROUPS, field_count, points), order.reshape(WAVES, 1))


def legendre_kernel(first_ref, recv_ref, leg_ref, out_ref, operand):
    slot = pl.program_id(0)
    lane = lax.broadcasted_iota(jnp.int32, (16, LANE), 1)
    odd32 = (lane // 32) % 2 == 1
    high64 = lane >= 64

    def regroup(tiles):
        a, b, c, d = tiles
        ab0 = jnp.where(odd32, pltpu.roll(b, 32, 1), a)
        ab1 = jnp.where(odd32, b, pltpu.roll(a, 96, 1))
        cd0 = jnp.where(odd32, pltpu.roll(d, 32, 1), c)
        cd1 = jnp.where(odd32, d, pltpu.roll(c, 96, 1))
        return (
            jnp.where(high64, pltpu.roll(cd0, 64, 1), ab0),
            jnp.where(high64, pltpu.roll(cd1, 64, 1), ab1),
            jnp.where(high64, cd0, pltpu.roll(ab0, 64, 1)),
            jnp.where(high64, cd1, pltpu.roll(ab1, 64, 1)),
        )

    half = recv_ref.shape[0] // 2

    def pair(w, carry):
        north = regroup([recv_ref[w, v, 0].astype(jnp.float32) for v in range(4)])
        south = regroup([recv_ref[half + w, v, 0].astype(jnp.float32) for v in range(4)])
        for t in range(0, 4, 2):
            top = pl.multiple_of(w * 32 + t * 8, 16)
            sums = [north[t + e] + south[t + e] for e in range(2)]
            differences = [north[t + e] - south[t + e] for e in range(2)]
            for side in range(2):
                rows = slice(side * 8, side * 8 + 8)
                for kind, both in enumerate((sums, differences)):
                    at = (side * 2 + kind) * LANE
                    operand[pl.ds(top, 16), at : at + LANE] = jnp.concatenate(
                        [both[0][rows], both[1][rows]], axis=0
                    ).astype(jnp.bfloat16)
        return carry

    lax.fori_loop(0, half, pair, 0)
    first_count = first_ref[slot]
    columns = leg_ref.shape[2]
    product = lax.dot_general(
        operand[...], leg_ref[0], (((0,), (0,)), ((), ())), preferred_element_type=jnp.float32
    )
    column = lax.broadcasted_iota(jnp.int32, (1, columns), 1)
    in_first = column < first_count
    degree = jnp.where(in_first, column, column - first_count)
    even = degree % 2 == 0
    for v in range(4):
        for i in range(2):
            top = v * 32 + i * 16
            s0, a0, s1, a1 = (product[k * LANE + top : k * LANE + top + 16] for k in range(4))
            chosen = jnp.where(in_first, jnp.where(even, s0, a0), jnp.where(even, s1, a1))
            out_ref[0, i, v * 16 : v * 16 + 16, :] = chosen


def legendre_all(received, legendre, local_pairs, wa_count, vert_count):
    slot_count, lat_pairs, columns = legendre.shape
    field_count = 16 * vert_count
    first_count = (WAVES - local_pairs).astype(jnp.int32)
    shaped = received.reshape(wa_count, vert_count, slot_count, 16, LANE)
    return pl.pallas_call(
        legendre_kernel,
        grid=(slot_count,),
        in_specs=[
            pl.BlockSpec(memory_space=pltpu.SMEM),
            pl.BlockSpec((wa_count, vert_count, 1, 16, LANE), lambda s: (0, 0, s, 0, 0)),
            pl.BlockSpec((1, lat_pairs, columns), lambda s: (s, 0, 0)),
        ],
        out_specs=pl.BlockSpec((1, 2, field_count, columns), lambda s: (s, 0, 0, 0)),
        out_shape=jax.ShapeDtypeStruct((slot_count, 2, field_count, columns), jnp.float32),
        scratch_shapes=[pltpu.VMEM((lat_pairs, 4 * LANE), jnp.bfloat16)],
        compiler_params=pltpu.CompilerParams(vmem_limit_bytes=48 * 2**20),
        name="legendre",
    )(first_count, shaped, legendre)


def body(grid_values, row_length, pair_order, legendre):
    wa_count = lax.axis_size("wa")
    vert_count = lax.axis_size("vert")
    device_total = wa_count * vert_count
    order = jnp.stack([pair_order, TRUNC - pair_order], axis=1).reshape(-1)
    sent = fourier_all(grid_values, row_length, order, device_total)
    received = lax.all_to_all(sent, ("wa", "vert"), split_axis=0, concat_axis=0, tiled=True)
    slot_count = legendre.shape[0]
    owner_idx = lax.axis_index("wa") * vert_count + lax.axis_index("vert")
    local_pairs = lax.dynamic_slice_in_dim(pair_order, owner_idx * slot_count, slot_count)
    return legendre_all(received, legendre, local_pairs, wa_count, vert_count)


def solution(mesh):
    placed = (P("wa", "vert", None), P("wa"), P(), P(("wa", "vert"), None, None))
    return jax.shard_map(
        body,
        mesh=mesh,
        in_specs=placed,
        out_specs=P(("wa", "vert"), None, None, None),
        check_vma=False,
    )
```

```python
import functools
import math

import jax
import jax.numpy as jnp
from jax import lax
from jax.experimental import pallas as pl
from jax.experimental.pallas import tpu as pltpu
from jax.sharding import PartitionSpec as P

TRUNC = 1279
SUB = 256
LPAD = 5376
WAVES = TRUNC + 1
CLASS = WAVES // 4
CPAD = 384
LANE = 128
CHUNKS = 11
BLOCKS = 6
GROUPS = 8
SPAN = 4
ORDER = 5
STRIDE = 37
PART = 640


def sincos(turns):
    quarter = turns * 4.0
    near = jnp.floor(quarter + 0.5)
    f = quarter - near
    f2 = f * f
    h = math.pi / 2
    s = f * (h + f2 * (-(h**3) / 6 + f2 * (h**5 / 120 + f2 * (-(h**7) / 5040 + f2 * (h**9 / 362880)))))
    c = 1.0 + f2 * (
        -(h**2) / 2 + f2 * (h**4 / 24 + f2 * (-(h**6) / 720 + f2 * (h**8 / 40320 - f2 * (h**10 / 3628800))))
    )
    which = near - 4.0 * jnp.floor(near * 0.25)
    odd = (which == 1.0) | (which == 3.0)
    cos_out = jnp.where(odd, s, c)
    sin_out = jnp.where(odd, c, s)
    cos_out = jnp.where((which == 1.0) | (which == 2.0), -cos_out, cos_out)
    sin_out = jnp.where(which >= 2.0, -sin_out, sin_out)
    return cos_out, sin_out


def turns_of(product, n_float, inv_n):
    return (product - jnp.floor(product * inv_n) * n_float) * inv_n


def iota_f(shape, dim):
    return lax.broadcasted_iota(jnp.int32, shape, dim).astype(jnp.float32)


def fold_kernel(length_ref, grid_ref, even_ref, rest_ref, twiddle):
    g = pl.program_id(0)

    @pl.when(g == 0)
    def _():
        def eight_rows(block, carry):
            sub = lax.broadcasted_iota(jnp.int32, (8, LANE), 0)
            n8 = jnp.zeros((8, LANE), jnp.int32)
            for e in range(8):
                n8 = jnp.where(sub == e, length_ref[block * 8 + e] // 4, n8)
            inv8 = 0.25 / n8.astype(jnp.float32)
            for j in range(CHUNKS):
                k = lax.broadcasted_iota(jnp.int32, (8, LANE), 1) + j * LANE
                c1, s1 = sincos(k.astype(jnp.float32) * inv8)
                c2 = c1 * c1 - s1 * s1
                s2 = 2.0 * c1 * s1
                c3 = c2 * c1 - s2 * s1
                s3 = s2 * c1 + c2 * s1
                for which, v in enumerate((c1, s1, c2, s2, c3, s3)):
                    for e in range(8):
                        twiddle[block * 8 + e, which : which + 1, j * LANE : (j + 1) * LANE] = v[e : e + 1]
            return carry

        lax.fori_loop(0, twiddle.shape[0] // 8, eight_rows, 0)

    lane = lax.broadcasted_iota(jnp.int32, (16, LANE), 1)
    zero = jnp.zeros((16, LANE), jnp.bfloat16)

    def one_row(t, carry):
        row = t * GROUPS + g
        n = length_ref[row] // 4
        starts = []
        for part in range(4):
            start = n * part
            whole = start // LANE
            shift = start - whole * LANE
            starts.append((whole, shift, lax.rem(LANE - shift, LANE)))

        def piece(part, j):
            whole, shift, back = starts[part]
            at = pl.multiple_of((whole + j) * LANE, LANE)
            value = grid_ref[t, 0, :, pl.ds(at, LANE)].astype(jnp.float32)
            return pltpu.roll(value, back, 1) if part else value

        held = [piece(part, 0) for part in range(4)]
        for j in range(CHUNKS):
            inside = lane + j * LANE < n
            quarter = []
            for part in range(4):
                value = held[part]
                following = piece(part, j + 1) if part or j + 1 < CHUNKS else None
                if part:
                    value = jnp.where(lane < LANE - starts[part][1], value, following)
                held[part] = following
                quarter.append(jnp.where(inside, value, 0.0))
            c1, s1, c2, s2, c3, s3 = (
                twiddle[row, which : which + 1, j * LANE : (j + 1) * LANE] for which in range(6)
            )
            qa, qb, qc, qd = quarter
            even = qa + qc
            even_other = qb + qd
            re = qa - qc
            im = qd - qb
            h2 = even - even_other
            q = j // 2
            at = (j % 2) * LANE
            even_ref[t, 0, q * 16 : q * 16 + 16, at : at + LANE] = (even + even_other).astype(jnp.bfloat16)
            values = (
                (re * c1 + im * s1, im * c1 - re * s1),
                (h2 * c2, -(h2 * s2)),
                (re * c3 - im * s3, -(im * c3 + re * s3)),
            )
            for r, (zr, zi) in enumerate(values):
                top = (r * BLOCKS + q) * 16
                rest_ref[t, 0, top : top + 16, at : at + LANE] = zr.astype(jnp.bfloat16)
                rest_ref[t, 0, top : top + 16, SUB + at : SUB + at + LANE] = zi.astype(jnp.bfloat16)
        for j in range(CHUNKS, 2 * BLOCKS):
            q = j // 2
            at = (j % 2) * LANE
            even_ref[t, 0, q * 16 : q * 16 + 16, at : at + LANE] = zero
            for r in range(3):
                top = (r * BLOCKS + q) * 16
                rest_ref[t, 0, top : top + 16, at : at + LANE] = zero
                rest_ref[t, 0, top : top + 16, SUB + at : SUB + at + LANE] = zero
        return carry

    lax.fori_loop(0, SPAN, one_row, 0)


def fold_all(grid_values, row_length):
    row_total, field_count, points = grid_values.shape
    return pl.pallas_call(
        fold_kernel,
        grid=(GROUPS,),
        in_specs=[
            pl.BlockSpec(memory_space=pltpu.SMEM),
            pl.BlockSpec((SPAN, 1, field_count, points), lambda g: (0, g, 0, 0)),
        ],
        out_specs=[
            pl.BlockSpec((SPAN, 1, BLOCKS * 16, SUB), lambda g: (0, g, 0, 0)),
            pl.BlockSpec((SPAN, 1, 3 * BLOCKS * 16, 2 * SUB), lambda g: (0, g, 0, 0)),
        ],
        out_shape=[
            jax.ShapeDtypeStruct((SPAN, GROUPS, BLOCKS * 16, SUB), jnp.bfloat16),
            jax.ShapeDtypeStruct((SPAN, GROUPS, 3 * BLOCKS * 16, 2 * SUB), jnp.bfloat16),
        ],
        scratch_shapes=[pltpu.VMEM((row_total, 8, CHUNKS * LANE), jnp.float32)],
        compiler_params=pltpu.CompilerParams(vmem_limit_bytes=60 * 2**20),
        name="fold",
    )(row_length, grid_values.reshape(SPAN, GROUPS, field_count, points))


def fourier_kernel(
    length_ref,
    order_ref,
    even_ref,
    rest_ref,
    out_ref,
    rhs,
    small,
    onehot,
    rows,
    spread,
    sending,
    landing,
    local_sem,
    send_sem,
    recv_sem,
):
    g = pl.program_id(0)
    vert_count = lax.axis_size("vert")
    total = lax.axis_size("wa") * vert_count
    me = lax.axis_index("wa") * vert_count + lax.axis_index("vert")
    dest_rows = WAVES * GROUPS // total
    per_dest = WAVES // total

    def place(device):
        return (device // vert_count, lax.rem(device, vert_count))

    @pl.when(g == 0)
    def _():
        barrier = pltpu.get_barrier_semaphore()

        def greet(i, carry):
            other = lax.rem(me + i, total)
            pl.semaphore_signal(barrier, 1, device_id=place(other), device_id_type=pl.DeviceIdType.MESH)
            return carry

        lax.fori_loop(1, total, greet, 0)
        for c in range(per_dest):
            pair = order_ref[:, c // 2 : c // 2 + 1]
            target = TRUNC - pair if c % 2 else pair
            for r in range(4):
                wave = lax.broadcasted_iota(jnp.int32, (total, CPAD), 1) * 4 + r
                wave = jnp.where(wave < WAVES, wave, -1)
                onehot[c * total : (c + 1) * total, r * CPAD : (r + 1) * CPAD] = (
                    (wave == target).astype(jnp.float32).astype(jnp.bfloat16)
                )

    def prepare(t):
        slot = t % 2
        n = jnp.full((8, CPAD), length_ref[t * GROUPS + g] // 4, jnp.int32)
        n_float = n.astype(jnp.float32)
        inv_n = 1.0 / n_float
        u = iota_f((8, CPAD), 1)
        low = iota_f((8, CPAD), 0)
        mixed = jnp.where(low == 0.0, 8.0, jnp.where(low == 1.0, 128.0, 256.0 * (low - 1.0)))
        cb, sb = sincos(turns_of(low * u, n_float, inv_n))
        ct, st = sincos(turns_of(low * 16.0 * u, n_float, inv_n))
        cm, sm = sincos(turns_of(mixed * u, n_float, inv_n))
        small[slot, 0, :8] = ct
        small[slot, 1, :8] = st
        small[slot, 0, 16:] = cm
        small[slot, 1, 16:] = sm
        c8, s8 = small[slot, 0, 16:17, :], small[slot, 1, 16:17, :]
        c128, s128 = small[slot, 0, 17:18, :], small[slot, 1, 17:18, :]
        small[slot, 0, 8:16] = ct * c128 - st * s128
        small[slot, 1, 8:16] = st * c128 + ct * s128
        base = ((cb, sb), (cb * c8 - sb * s8, sb * c8 + cb * s8))
        for a in range(16):
            ca = small[slot, 0, a : a + 1, :]
            sa = small[slot, 1, a : a + 1, :]
            c = jnp.concatenate([x * ca - y * sa for x, y in base], axis=0)
            s = jnp.concatenate([y * ca + x * sa for x, y in base], axis=0)
            c16 = c.astype(jnp.bfloat16)
            s16 = s.astype(jnp.bfloat16)
            rhs[slot, a * 16 : a * 16 + 16, :CPAD] = c16
            rhs[slot, a * 16 : a * 16 + 16, CPAD:] = -s16
            rhs[slot, SUB + a * 16 : SUB + a * 16 + 16, :CPAD] = s16
            rhs[slot, SUB + a * 16 : SUB + a * 16 + 16, CPAD:] = c16

    paired = (g == 1) | (g == 3) | (g == 6)

    def finish(t, sums):
        slot = t % 2
        length = jnp.full((1, CPAD), length_ref[t * GROUPS + g], jnp.int32)
        scale = 1.0 / jnp.sqrt(length.astype(jnp.float32))
        column = lax.broadcasted_iota(jnp.int32, (1, CPAD), 1)
        lane_top = pl.multiple_of(jnp.where(paired, LANE, 0) + t * 32, 32)
        for r in range(4):
            part_sum, first = (sums[0], 0) if r == 0 else (sums[1], (r - 1) * 96)
            real = part_sum[first : first + 16, :CPAD]
            imag = part_sum[first : first + 16, CPAD:]
            for q in range(1, BLOCKS):
                top = first + q * 16
                pr = part_sum[top : top + 16, :CPAD]
                pi = part_sum[top : top + 16, CPAD:]
                c = small[slot, 0, 17 + q : 18 + q, :]
                s = small[slot, 1, 17 + q : 18 + q, :]
                real = real + (pr * c + pi * s)
                imag = imag + (pi * c - pr * s)
            wave = column * 4 + r
            keep = jnp.where((wave * 2 <= length - 1) & (column < CLASS), scale, 0.0)
            rows[pl.ds(lane_top, 16), r * CPAD : (r + 1) * CPAD] = (real * keep).astype(jnp.bfloat16)
            rows[pl.ds(lane_top + 16, 16), r * CPAD : (r + 1) * CPAD] = (imag * keep).astype(jnp.bfloat16)

    prepare(0)
    for t in range(SPAN):
        sums = (
            jnp.dot(even_ref[t, 0], rhs[t % 2, :SUB], preferred_element_type=jnp.float32),
            jnp.dot(rest_ref[t, 0], rhs[t % 2], preferred_element_type=jnp.float32),
        )
        if t + 1 < SPAN:
            prepare(t + 1)
        finish(t, sums)

    def order(count):
        for c0 in range(0, per_dest, ORDER):
            picked = lax.dot_general(
                onehot[c0 * total : (c0 + ORDER) * total, :],
                rows[: count * LANE, :],
                (((1,), (1,)), ((), ())),
                preferred_element_type=jnp.float32,
            )
            for c in range(ORDER):
                for e in range(count):
                    at = (g - count + 1 + e) * per_dest + c0 + c
                    spread[pl.ds(at, total, stride=dest_rows), :] = picked[
                        c * total : (c + 1) * total, e * LANE : (e + 1) * LANE
                    ]

    pl.when(paired)(lambda: order(2))
    pl.when((g == 4) | (g == 7))(lambda: order(1))

    @pl.when(paired | (g == 4) | (g == 7))
    def _():
        tile = (5 * (g + 1)) // 8 - 1

        def convert(d, carry):
            sending[tile, d] = spread[pl.ds(pl.multiple_of(d * dest_rows + tile * 16, 16), 16), :].astype(jnp.bfloat16)
            return carry

        lax.fori_loop(0, total, convert, 0, unroll=8)

        @pl.when(g == 1)
        def _():
            pl.semaphore_wait(pltpu.get_barrier_semaphore(), total - 1)

        pltpu.make_async_copy(sending.at[tile, me], landing.at[tile, me], local_sem.at[tile]).start()

        def send(i, carry):
            other = lax.rem(me + i * STRIDE, total)
            pltpu.make_async_remote_copy(
                sending.at[tile, other],
                landing.at[tile, me],
                send_sem.at[tile],
                recv_sem.at[tile],
                device_id=place(other),
                device_id_type=pl.DeviceIdType.MESH,
            ).start()
            return carry

        lax.fori_loop(1, total, send, 0)

    @pl.when(g == GROUPS - 1)
    def _():
        tiles = out_ref.shape[0]
        others = pl.ds(0, total - 1)
        for tile in range(tiles):
            pltpu.make_async_copy(sending.at[tile, me], landing.at[tile, me], local_sem.at[tile]).wait()
            pltpu.make_async_copy(sending.at[tile, others], landing.at[tile, others], recv_sem.at[tile]).wait()
            pltpu.make_async_copy(landing.at[tile], out_ref.at[tile], local_sem.at[tile]).start()
        for tile in range(tiles):
            pltpu.make_async_copy(sending.at[tile, others], landing.at[tile, others], send_sem.at[tile]).wait()
            pltpu.make_async_copy(landing.at[tile], out_ref.at[tile], local_sem.at[tile]).wait()


def fourier_all(row_length, pair_order, even, rest, device_total):
    tiles = WAVES * GROUPS // device_total // 16
    return pl.pallas_call(
        fourier_kernel,
        grid=(GROUPS,),
        in_specs=[
            pl.BlockSpec(memory_space=pltpu.SMEM),
            pl.BlockSpec((device_total, pair_order.shape[0] // device_total), lambda g: (0, 0)),
            pl.BlockSpec((SPAN, 1) + even.shape[2:], lambda g: (0, g, 0, 0)),
            pl.BlockSpec((SPAN, 1) + rest.shape[2:], lambda g: (0, g, 0, 0)),
        ],
        out_specs=pl.BlockSpec(memory_space=pl.ANY),
        out_shape=jax.ShapeDtypeStruct((tiles, device_total, 16, LANE), jnp.bfloat16),
        scratch_shapes=[
            pltpu.VMEM((2, 2 * SUB, 2 * CPAD), jnp.bfloat16),
            pltpu.VMEM((2, 2, 24, CPAD), jnp.float32),
            pltpu.VMEM((WAVES, 4 * CPAD), jnp.bfloat16),
            pltpu.VMEM((2 * LANE, 4 * CPAD), jnp.bfloat16),
            pltpu.VMEM((WAVES * GROUPS, LANE), jnp.float32),
            pltpu.VMEM((tiles, device_total, 16, LANE), jnp.bfloat16),
            pltpu.VMEM((tiles, device_total, 16, LANE), jnp.bfloat16),
            pltpu.SemaphoreType.DMA((tiles,)),
            pltpu.SemaphoreType.DMA((tiles,)),
            pltpu.SemaphoreType.DMA((tiles,)),
        ],
        compiler_params=pltpu.CompilerParams(
            vmem_limit_bytes=60 * 2**20, collective_id=0, has_side_effects=True
        ),
        name="fourier",
    )(row_length, pair_order.reshape(device_total, -1), even, rest)


def legendre_kernel(pair_ref, recv_ref, leg_ref, out_ref, operand, loose):
    slot = pl.program_id(0)
    owner = lax.axis_index("wa") * lax.axis_size("vert") + lax.axis_index("vert")

    @pl.when(slot == 0)
    def _():
        lane = lax.broadcasted_iota(jnp.int32, (8, LANE), 1)
        odd32 = (lane // 32) % 2 == 1
        high64 = lane >= 64
        per_dest = loose.shape[2] // GROUPS
        half = recv_ref.shape[1] // 2

        def regroup(tiles):
            a, b, c, d = tiles
            ab0 = jnp.where(odd32, pltpu.roll(b, 32, 1), a)
            ab1 = jnp.where(odd32, b, pltpu.roll(a, 96, 1))
            cd0 = jnp.where(odd32, pltpu.roll(d, 32, 1), c)
            cd1 = jnp.where(odd32, d, pltpu.roll(c, 96, 1))
            return (
                jnp.where(high64, pltpu.roll(cd0, 64, 1), ab0),
                jnp.where(high64, pltpu.roll(cd1, 64, 1), ab1),
                jnp.where(high64, cd0, pltpu.roll(ab0, 64, 1)),
                jnp.where(high64, cd1, pltpu.roll(ab1, 64, 1)),
            )

        def pair(w, carry):
            for side in range(2):
                for v in range(4):
                    for tile in range(recv_ref.shape[0]):
                        loose[side, v, tile * 16 : tile * 16 + 16, :] = recv_ref[tile, side * half + w, v].astype(
                            jnp.float32
                        )
            for col in range(per_dest):
                north, south = (
                    regroup([loose[side, v, pl.ds(col, 8, stride=per_dest), :] for v in range(4)]) for side in range(2)
                )
                for t in range(0, 4, 2):
                    top = pl.multiple_of(w * 32 + t * 8, 16)
                    sums = [north[t + e] + south[t + e] for e in range(2)]
                    differences = [north[t + e] - south[t + e] for e in range(2)]
                    for kind, both in enumerate((sums, differences)):
                        at = ((col % 2) * 2 + kind) * LANE
                        operand[col // 2, pl.ds(top, 16), at : at + LANE] = jnp.concatenate(both, axis=0).astype(
                            jnp.bfloat16
                        )
            return carry

        lax.fori_loop(0, half, pair, 0)

    first_count = WAVES - pair_ref[owner * pl.num_programs(0) + slot]
    columns = leg_ref.shape[1]
    whole = columns // LANE * LANE

    def choose(product, top, out_lanes):
        height = product.shape[0]
        column = lax.broadcasted_iota(jnp.int32, (height, LANE), 0) + top
        in_first = column < first_count
        degree = jnp.where(in_first, column, column - first_count)
        even = degree % 2 == 0
        s0, a0, s1, a1 = (product[:, k * LANE : (k + 1) * LANE] for k in range(4))
        chosen = jnp.where(in_first, jnp.where(even, s0, a0), jnp.where(even, s1, a1))
        turned = chosen.T
        for v in range(4):
            for i in range(2):
                at = v * 32 + i * 16
                out_ref[0, i, v * 16 : v * 16 + 16, out_lanes] = turned[at : at + 16]

    for start in range(0, whole, PART):
        product = jnp.dot(
            leg_ref[0, start : start + PART, :], operand[slot], preferred_element_type=jnp.float32
        )
        for top in range(0, PART, LANE):
            choose(product[top : top + LANE], start + top, slice(start + top, start + top + LANE))
    last = leg_ref[0, whole:columns, :]
    product = jnp.dot(
        jnp.broadcast_to(last, (16, last.shape[1])), operand[slot], preferred_element_type=jnp.float32
    )
    column = jnp.zeros((16, LANE), jnp.int32) + whole
    in_first = column < first_count
    degree = jnp.where(in_first, column, column - first_count)
    even = degree % 2 == 0
    s0, a0, s1, a1 = (product[:, k * LANE : (k + 1) * LANE] for k in range(4))
    chosen = jnp.where(in_first, jnp.where(even, s0, a0), jnp.where(even, s1, a1))
    turned = jnp.broadcast_to(chosen[:1], (LANE, LANE)).T
    for v in range(4):
        for i in range(2):
            at = v * 32 + i * 16
            out_ref[0, i, v * 16 : v * 16 + 16, whole:columns] = turned[at : at + 16, : columns - whole]


def legendre_all(received, legendre, pair_order, wa_count, vert_count):
    slot_count, lat_pairs, columns = legendre.shape
    field_count = 16 * vert_count
    tiles = received.shape[0]
    turned = jnp.swapaxes(legendre, 1, 2)
    shaped = received.reshape(tiles, wa_count, vert_count, 16, LANE)
    return pl.pallas_call(
        legendre_kernel,
        grid=(slot_count,),
        in_specs=[
            pl.BlockSpec(memory_space=pltpu.SMEM),
            pl.BlockSpec(shaped.shape, lambda s: (0, 0, 0, 0, 0)),
            pl.BlockSpec((1, columns, lat_pairs), lambda s: (s, 0, 0)),
        ],
        out_specs=pl.BlockSpec((1, 2, field_count, columns), lambda s: (s, 0, 0, 0)),
        out_shape=jax.ShapeDtypeStruct((slot_count, 2, field_count, columns), jnp.float32),
        scratch_shapes=[
            pltpu.VMEM((slot_count, lat_pairs, 4 * LANE), jnp.bfloat16),
            pltpu.VMEM((2, vert_count, tiles * 16, LANE), jnp.float32),
        ],
        compiler_params=pltpu.CompilerParams(vmem_limit_bytes=60 * 2**20),
        name="legendre",
    )(pair_order, shaped, turned)


def body(grid_values, row_length, pair_order, legendre):
    wa_count = lax.axis_size("wa")
    vert_count = lax.axis_size("vert")
    device_total = wa_count * vert_count
    even, rest = fold_all(grid_values, row_length)
    received = fourier_all(row_length, pair_order, even, rest, device_total)
    return legendre_all(received, legendre, pair_order, wa_count, vert_count)


def solution(mesh):
    placed = (P("wa", "vert", None), P("wa"), P(), P(("wa", "vert"), None, None))
    return jax.shard_map(
        body,
        mesh=mesh,
        in_specs=placed,
        out_specs=P(("wa", "vert"), None, None, None),
        check_vma=False,
    )
```

```python
import functools
import math

import jax
import jax.numpy as jnp
from jax import lax
from jax.experimental import pallas as pl
from jax.experimental.pallas import tpu as pltpu
from jax.sharding import PartitionSpec as P

TRUNC = 1279
SUB = 256
LPAD = 5376
WAVES = TRUNC + 1
CLASS = WAVES // 4
CPAD = 384
LANE = 128
CHUNKS = 11
BLOCKS = 6
GROUPS = 8
SPAN = 4
ORDER = 5
STRIDE = 13
PART = 640


def sincos(turns):
    quarter = turns * 4.0
    near = jnp.floor(quarter + 0.5)
    f = quarter - near
    f2 = f * f
    h = math.pi / 2
    s = f * (h + f2 * (-(h**3) / 6 + f2 * (h**5 / 120 + f2 * (-(h**7) / 5040 + f2 * (h**9 / 362880)))))
    c = 1.0 + f2 * (
        -(h**2) / 2 + f2 * (h**4 / 24 + f2 * (-(h**6) / 720 + f2 * (h**8 / 40320 - f2 * (h**10 / 3628800))))
    )
    which = near - 4.0 * jnp.floor(near * 0.25)
    odd = (which == 1.0) | (which == 3.0)
    cos_out = jnp.where(odd, s, c)
    sin_out = jnp.where(odd, c, s)
    cos_out = jnp.where((which == 1.0) | (which == 2.0), -cos_out, cos_out)
    sin_out = jnp.where(which >= 2.0, -sin_out, sin_out)
    return cos_out, sin_out


def turns_of(product, n_float, inv_n):
    return (product - jnp.floor(product * inv_n) * n_float) * inv_n


def iota_f(shape, dim):
    return lax.broadcasted_iota(jnp.int32, shape, dim).astype(jnp.float32)


def fold_kernel(length_ref, grid_ref, even_ref, rest_ref, twiddle):
    g = pl.program_id(0)

    @pl.when(g == 0)
    def _():
        def eight_rows(block, carry):
            sub = lax.broadcasted_iota(jnp.int32, (8, LANE), 0)
            n8 = jnp.zeros((8, LANE), jnp.int32)
            for e in range(8):
                n8 = jnp.where(sub == e, length_ref[block * 8 + e] // 4, n8)
            inv8 = 0.25 / n8.astype(jnp.float32)
            for j in range(CHUNKS):
                k = lax.broadcasted_iota(jnp.int32, (8, LANE), 1) + j * LANE
                c1, s1 = sincos(k.astype(jnp.float32) * inv8)
                c2 = c1 * c1 - s1 * s1
                s2 = 2.0 * c1 * s1
                c3 = c2 * c1 - s2 * s1
                s3 = s2 * c1 + c2 * s1
                for which, v in enumerate((c1, s1, c2, s2, c3, s3)):
                    for e in range(8):
                        twiddle[block * 8 + e, which : which + 1, j * LANE : (j + 1) * LANE] = v[e : e + 1]
            return carry

        lax.fori_loop(0, twiddle.shape[0] // 8, eight_rows, 0)

    lane = lax.broadcasted_iota(jnp.int32, (16, LANE), 1)
    zero = jnp.zeros((16, LANE), jnp.bfloat16)

    def one_row(t, carry):
        row = t * GROUPS + g
        n = length_ref[row] // 4
        starts = []
        for part in range(4):
            start = n * part
            whole = start // LANE
            shift = start - whole * LANE
            starts.append((whole, shift, lax.rem(LANE - shift, LANE)))

        def piece(part, j):
            whole, shift, back = starts[part]
            at = pl.multiple_of((whole + j) * LANE, LANE)
            value = grid_ref[t, 0, :, pl.ds(at, LANE)].astype(jnp.float32)
            return pltpu.roll(value, back, 1) if part else value

        held = [piece(part, 0) for part in range(4)]
        for j in range(CHUNKS):
            inside = lane + j * LANE < n
            quarter = []
            for part in range(4):
                value = held[part]
                following = piece(part, j + 1) if part or j + 1 < CHUNKS else None
                if part:
                    value = jnp.where(lane < LANE - starts[part][1], value, following)
                held[part] = following
                quarter.append(jnp.where(inside, value, 0.0))
            c1, s1, c2, s2, c3, s3 = (
                twiddle[row, which : which + 1, j * LANE : (j + 1) * LANE] for which in range(6)
            )
            qa, qb, qc, qd = quarter
            even = qa + qc
            even_other = qb + qd
            re = qa - qc
            im = qd - qb
            h2 = even - even_other
            q = j // 2
            at = (j % 2) * LANE
            even_ref[t, 0, q * 16 : q * 16 + 16, at : at + LANE] = (even + even_other).astype(jnp.bfloat16)
            values = (
                (re * c1 + im * s1, im * c1 - re * s1),
                (h2 * c2, -(h2 * s2)),
                (re * c3 - im * s3, -(im * c3 + re * s3)),
            )
            for r, (zr, zi) in enumerate(values):
                top = (r * BLOCKS + q) * 16
                rest_ref[t, 0, top : top + 16, at : at + LANE] = zr.astype(jnp.bfloat16)
                rest_ref[t, 0, top : top + 16, SUB + at : SUB + at + LANE] = zi.astype(jnp.bfloat16)
        for j in range(CHUNKS, 2 * BLOCKS):
            q = j // 2
            at = (j % 2) * LANE
            even_ref[t, 0, q * 16 : q * 16 + 16, at : at + LANE] = zero
            for r in range(3):
                top = (r * BLOCKS + q) * 16
                rest_ref[t, 0, top : top + 16, at : at + LANE] = zero
                rest_ref[t, 0, top : top + 16, SUB + at : SUB + at + LANE] = zero
        return carry

    lax.fori_loop(0, SPAN, one_row, 0)


def fold_all(grid_values, row_length):
    row_total, field_count, points = grid_values.shape
    return pl.pallas_call(
        fold_kernel,
        grid=(GROUPS,),
        in_specs=[
            pl.BlockSpec(memory_space=pltpu.SMEM),
            pl.BlockSpec((SPAN, 1, field_count, points), lambda g: (0, g, 0, 0)),
        ],
        out_specs=[
            pl.BlockSpec((SPAN, 1, BLOCKS * 16, SUB), lambda g: (0, g, 0, 0)),
            pl.BlockSpec((SPAN, 1, 3 * BLOCKS * 16, 2 * SUB), lambda g: (0, g, 0, 0)),
        ],
        out_shape=[
            jax.ShapeDtypeStruct((SPAN, GROUPS, BLOCKS * 16, SUB), jnp.bfloat16),
            jax.ShapeDtypeStruct((SPAN, GROUPS, 3 * BLOCKS * 16, 2 * SUB), jnp.bfloat16),
        ],
        scratch_shapes=[pltpu.VMEM((row_total, 8, CHUNKS * LANE), jnp.float32)],
        compiler_params=pltpu.CompilerParams(vmem_limit_bytes=16 * 2**20),
        name="fold",
    )(row_length, grid_values.reshape(SPAN, GROUPS, field_count, points))


def fourier_kernel(
    length_ref,
    order_ref,
    even_ref,
    rest_ref,
    out_ref,
    rhs,
    small,
    onehot,
    rows,
    spread,
    sending,
    landing,
    local_sem,
    send_sem,
    recv_sem,
):
    g = pl.program_id(0)
    vert_count = lax.axis_size("vert")
    total = lax.axis_size("wa") * vert_count
    me = lax.axis_index("wa") * vert_count + lax.axis_index("vert")
    dest_rows = WAVES * GROUPS // total
    per_dest = WAVES // total

    def place(device):
        return (device // vert_count, lax.rem(device, vert_count))

    @pl.when(g == 0)
    def _():
        barrier = pltpu.get_barrier_semaphore()

        def greet(i, carry):
            other = lax.rem(me + i, total)
            pl.semaphore_signal(barrier, 1, device_id=place(other), device_id_type=pl.DeviceIdType.MESH)
            return carry

        lax.fori_loop(1, total, greet, 0)
        for c in range(per_dest):
            pair = order_ref[:, c // 2 : c // 2 + 1]
            target = TRUNC - pair if c % 2 else pair
            for r in range(4):
                wave = lax.broadcasted_iota(jnp.int32, (total, CPAD), 1) * 4 + r
                wave = jnp.where(wave < WAVES, wave, -1)
                onehot[c * total : (c + 1) * total, r * CPAD : (r + 1) * CPAD] = (
                    (wave == target).astype(jnp.float32).astype(jnp.bfloat16)
                )

    def prepare(t):
        slot = t % 2
        n = jnp.full((8, CPAD), length_ref[t * GROUPS + g] // 4, jnp.int32)
        n_float = n.astype(jnp.float32)
        inv_n = 1.0 / n_float
        u = iota_f((8, CPAD), 1)
        low = iota_f((8, CPAD), 0)
        mixed = jnp.where(low == 0.0, 8.0, jnp.where(low == 1.0, 128.0, 256.0 * (low - 1.0)))
        cb, sb = sincos(turns_of(low * u, n_float, inv_n))
        ct, st = sincos(turns_of(low * 16.0 * u, n_float, inv_n))
        cm, sm = sincos(turns_of(mixed * u, n_float, inv_n))
        small[slot, 0, :8] = ct
        small[slot, 1, :8] = st
        small[slot, 0, 16:] = cm
        small[slot, 1, 16:] = sm
        c8, s8 = small[slot, 0, 16:17, :], small[slot, 1, 16:17, :]
        c128, s128 = small[slot, 0, 17:18, :], small[slot, 1, 17:18, :]
        small[slot, 0, 8:16] = ct * c128 - st * s128
        small[slot, 1, 8:16] = st * c128 + ct * s128
        base = ((cb, sb), (cb * c8 - sb * s8, sb * c8 + cb * s8))
        for a in range(16):
            ca = small[slot, 0, a : a + 1, :]
            sa = small[slot, 1, a : a + 1, :]
            c = jnp.concatenate([x * ca - y * sa for x, y in base], axis=0)
            s = jnp.concatenate([y * ca + x * sa for x, y in base], axis=0)
            c16 = c.astype(jnp.bfloat16)
            s16 = s.astype(jnp.bfloat16)
            rhs[slot, a * 16 : a * 16 + 16, :CPAD] = c16
            rhs[slot, a * 16 : a * 16 + 16, CPAD:] = -s16
            rhs[slot, SUB + a * 16 : SUB + a * 16 + 16, :CPAD] = s16
            rhs[slot, SUB + a * 16 : SUB + a * 16 + 16, CPAD:] = c16

    paired = (g == 1) | (g == 3) | (g == 6)

    def finish(t, sums):
        slot = t % 2
        length = jnp.full((1, CPAD), length_ref[t * GROUPS + g], jnp.int32)
        scale = 1.0 / jnp.sqrt(length.astype(jnp.float32))
        column = lax.broadcasted_iota(jnp.int32, (1, CPAD), 1)
        lane_top = pl.multiple_of(jnp.where(paired, LANE, 0) + t * 32, 32)
        for r in range(4):
            part_sum, first = (sums[0], 0) if r == 0 else (sums[1], (r - 1) * 96)
            real = part_sum[first : first + 16, :CPAD]
            imag = part_sum[first : first + 16, CPAD:]
            for q in range(1, BLOCKS):
                top = first + q * 16
                pr = part_sum[top : top + 16, :CPAD]
                pi = part_sum[top : top + 16, CPAD:]
                c = small[slot, 0, 17 + q : 18 + q, :]
                s = small[slot, 1, 17 + q : 18 + q, :]
                real = real + (pr * c + pi * s)
                imag = imag + (pi * c - pr * s)
            wave = column * 4 + r
            keep = jnp.where((wave * 2 <= length - 1) & (column < CLASS), scale, 0.0)
            rows[pl.ds(lane_top, 16), r * CPAD : (r + 1) * CPAD] = (real * keep).astype(jnp.bfloat16)
            rows[pl.ds(lane_top + 16, 16), r * CPAD : (r + 1) * CPAD] = (imag * keep).astype(jnp.bfloat16)

    prepare(0)
    for t in range(SPAN):
        sums = (
            jnp.dot(even_ref[t, 0], rhs[t % 2, :SUB], preferred_element_type=jnp.float32),
            jnp.dot(rest_ref[t, 0], rhs[t % 2], preferred_element_type=jnp.float32),
        )
        if t + 1 < SPAN:
            prepare(t + 1)
        finish(t, sums)

    def order(count):
        for c0 in range(0, per_dest, ORDER):
            picked = lax.dot_general(
                onehot[c0 * total : (c0 + ORDER) * total, :],
                rows[: count * LANE, :],
                (((1,), (1,)), ((), ())),
                preferred_element_type=jnp.float32,
            )
            for c in range(ORDER):
                for e in range(count):
                    at = (g - count + 1 + e) * per_dest + c0 + c
                    spread[pl.ds(at, total, stride=dest_rows), :] = picked[
                        c * total : (c + 1) * total, e * LANE : (e + 1) * LANE
                    ]

    pl.when(paired)(lambda: order(2))
    pl.when((g == 4) | (g == 7))(lambda: order(1))

    @pl.when(paired | (g == 4) | (g == 7))
    def _():
        tile = (5 * (g + 1)) // 8 - 1

        def convert(d, carry):
            sending[tile, d] = spread[pl.ds(pl.multiple_of(d * dest_rows + tile * 16, 16), 16), :].astype(jnp.bfloat16)
            return carry

        lax.fori_loop(0, total, convert, 0, unroll=8)

        @pl.when(g == 1)
        def _():
            pl.semaphore_wait(pltpu.get_barrier_semaphore(), total - 1)

        pltpu.make_async_copy(sending.at[tile, me], landing.at[tile, me], local_sem.at[tile]).start()

        wa_count = lax.axis_size("wa")
        wa, vert = lax.axis_index("wa"), lax.axis_index("vert")

        def send(to_wa, to_vert):
            pltpu.make_async_remote_copy(
                sending.at[tile, to_wa * vert_count + to_vert],
                landing.at[tile, me],
                send_sem.at[tile],
                recv_sem.at[tile],
                device_id=(to_wa, to_vert),
                device_id_type=pl.DeviceIdType.MESH,
            ).start()

        for i in range(1, vert_count):
            send(wa, lax.rem(vert + i, vert_count))

        def spoke(i, carry):
            to_wa = lax.rem(wa + i * STRIDE, wa_count)
            for to_vert in range(vert_count):
                send(to_wa, to_vert)
            return carry

        lax.fori_loop(1, wa_count, spoke, 0)

    @pl.when(g == GROUPS - 1)
    def _():
        tiles = out_ref.shape[0]
        others = pl.ds(0, total - 1)
        for tile in range(tiles):
            pltpu.make_async_copy(sending.at[tile, me], landing.at[tile, me], local_sem.at[tile]).wait()
            pltpu.make_async_copy(sending.at[tile, others], landing.at[tile, others], recv_sem.at[tile]).wait()
            pltpu.make_async_copy(landing.at[tile], out_ref.at[tile], local_sem.at[tile]).start()
        for tile in range(tiles):
            pltpu.make_async_copy(sending.at[tile, others], landing.at[tile, others], send_sem.at[tile]).wait()
            pltpu.make_async_copy(landing.at[tile], out_ref.at[tile], local_sem.at[tile]).wait()


def fourier_all(row_length, pair_order, even, rest, device_total):
    tiles = WAVES * GROUPS // device_total // 16
    return pl.pallas_call(
        fourier_kernel,
        grid=(GROUPS,),
        in_specs=[
            pl.BlockSpec(memory_space=pltpu.SMEM),
            pl.BlockSpec((device_total, pair_order.shape[0] // device_total), lambda g: (0, 0)),
            pl.BlockSpec((SPAN, 1) + even.shape[2:], lambda g: (0, g, 0, 0)),
            pl.BlockSpec((SPAN, 1) + rest.shape[2:], lambda g: (0, g, 0, 0)),
        ],
        out_specs=pl.BlockSpec(memory_space=pl.ANY),
        out_shape=jax.ShapeDtypeStruct((tiles, device_total, 16, LANE), jnp.bfloat16),
        scratch_shapes=[
            pltpu.VMEM((2, 2 * SUB, 2 * CPAD), jnp.bfloat16),
            pltpu.VMEM((2, 2, 24, CPAD), jnp.float32),
            pltpu.VMEM((WAVES, 4 * CPAD), jnp.bfloat16),
            pltpu.VMEM((2 * LANE, 4 * CPAD), jnp.bfloat16),
            pltpu.VMEM((WAVES * GROUPS, LANE), jnp.float32),
            pltpu.VMEM((tiles, device_total, 16, LANE), jnp.bfloat16),
            pltpu.VMEM((tiles, device_total, 16, LANE), jnp.bfloat16),
            pltpu.SemaphoreType.DMA((tiles,)),
            pltpu.SemaphoreType.DMA((tiles,)),
            pltpu.SemaphoreType.DMA((tiles,)),
        ],
        compiler_params=pltpu.CompilerParams(
            vmem_limit_bytes=34 * 2**20, collective_id=0, has_side_effects=True
        ),
        name="fourier",
    )(row_length, pair_order.reshape(device_total, -1), even, rest)


def legendre_kernel(pair_ref, recv_ref, leg_ref, out_ref, operand, loose):
    slot = pl.program_id(0)
    owner = lax.axis_index("wa") * lax.axis_size("vert") + lax.axis_index("vert")

    @pl.when(slot == 0)
    def _():
        lane = lax.broadcasted_iota(jnp.int32, (8, LANE), 1)
        odd32 = (lane // 32) % 2 == 1
        high64 = lane >= 64
        per_dest = loose.shape[2] // GROUPS
        half = recv_ref.shape[1] // 2

        def regroup(tiles):
            a, b, c, d = tiles
            ab0 = jnp.where(odd32, pltpu.roll(b, 32, 1), a)
            ab1 = jnp.where(odd32, b, pltpu.roll(a, 96, 1))
            cd0 = jnp.where(odd32, pltpu.roll(d, 32, 1), c)
            cd1 = jnp.where(odd32, d, pltpu.roll(c, 96, 1))
            return (
                jnp.where(high64, pltpu.roll(cd0, 64, 1), ab0),
                jnp.where(high64, pltpu.roll(cd1, 64, 1), ab1),
                jnp.where(high64, cd0, pltpu.roll(ab0, 64, 1)),
                jnp.where(high64, cd1, pltpu.roll(ab1, 64, 1)),
            )

        def pair(w, carry):
            for side in range(2):
                for v in range(4):
                    for tile in range(recv_ref.shape[0]):
                        loose[side, v, tile * 16 : tile * 16 + 16, :] = recv_ref[tile, side * half + w, v].astype(
                            jnp.float32
                        )
            for col in range(per_dest):
                north, south = (
                    regroup([loose[side, v, pl.ds(col, 8, stride=per_dest), :] for v in range(4)]) for side in range(2)
                )
                for t in range(0, 4, 2):
                    top = pl.multiple_of(w * 32 + t * 8, 16)
                    sums = [north[t + e] + south[t + e] for e in range(2)]
                    differences = [north[t + e] - south[t + e] for e in range(2)]
                    for kind, both in enumerate((sums, differences)):
                        at = ((col % 2) * 2 + kind) * LANE
                        operand[col // 2, pl.ds(top, 16), at : at + LANE] = jnp.concatenate(both, axis=0).astype(
                            jnp.bfloat16
                        )
            return carry

        lax.fori_loop(0, half, pair, 0)

    first_count = WAVES - pair_ref[owner * pl.num_programs(0) + slot]
    columns = leg_ref.shape[1]
    whole = columns // LANE * LANE

    def choose(product, top, out_lanes):
        height = product.shape[0]
        column = lax.broadcasted_iota(jnp.int32, (height, LANE), 0) + top
        in_first = column < first_count
        degree = jnp.where(in_first, column, column - first_count)
        even = degree % 2 == 0
        s0, a0, s1, a1 = (product[:, k * LANE : (k + 1) * LANE] for k in range(4))
        chosen = jnp.where(in_first, jnp.where(even, s0, a0), jnp.where(even, s1, a1))
        turned = chosen.T
        for v in range(4):
            for i in range(2):
                at = v * 32 + i * 16
                out_ref[0, i, v * 16 : v * 16 + 16, out_lanes] = turned[at : at + 16]

    for start in range(0, whole, PART):
        product = jnp.dot(
            leg_ref[0, start : start + PART, :], operand[slot], preferred_element_type=jnp.float32
        )
        for top in range(0, PART, LANE):
            choose(product[top : top + LANE], start + top, slice(start + top, start + top + LANE))
    last = leg_ref[0, whole:columns, :]
    product = jnp.dot(
        jnp.broadcast_to(last, (16, last.shape[1])), operand[slot], preferred_element_type=jnp.float32
    )
    column = jnp.zeros((16, LANE), jnp.int32) + whole
    in_first = column < first_count
    degree = jnp.where(in_first, column, column - first_count)
    even = degree % 2 == 0
    s0, a0, s1, a1 = (product[:, k * LANE : (k + 1) * LANE] for k in range(4))
    chosen = jnp.where(in_first, jnp.where(even, s0, a0), jnp.where(even, s1, a1))
    turned = jnp.broadcast_to(chosen[:1], (LANE, LANE)).T
    for v in range(4):
        for i in range(2):
            at = v * 32 + i * 16
            out_ref[0, i, v * 16 : v * 16 + 16, whole:columns] = turned[at : at + 16, : columns - whole]


def legendre_all(received, legendre, pair_order, wa_count, vert_count):
    slot_count, lat_pairs, columns = legendre.shape
    field_count = 16 * vert_count
    tiles = received.shape[0]
    turned = jnp.swapaxes(legendre, 1, 2)
    shaped = received.reshape(tiles, wa_count, vert_count, 16, LANE)
    return pl.pallas_call(
        legendre_kernel,
        grid=(slot_count,),
        in_specs=[
            pl.BlockSpec(memory_space=pltpu.SMEM),
            pl.BlockSpec(shaped.shape, lambda s: (0, 0, 0, 0, 0)),
            pl.BlockSpec((1, columns, lat_pairs), lambda s: (s, 0, 0)),
        ],
        out_specs=pl.BlockSpec((1, 2, field_count, columns), lambda s: (s, 0, 0, 0)),
        out_shape=jax.ShapeDtypeStruct((slot_count, 2, field_count, columns), jnp.float32),
        scratch_shapes=[
            pltpu.VMEM((slot_count, lat_pairs, 4 * LANE), jnp.bfloat16),
            pltpu.VMEM((2, vert_count, tiles * 16, LANE), jnp.float32),
        ],
        compiler_params=pltpu.CompilerParams(vmem_limit_bytes=24 * 2**20),
        name="legendre",
    )(pair_order, shaped, turned)


def body(grid_values, row_length, pair_order, legendre):
    wa_count = lax.axis_size("wa")
    vert_count = lax.axis_size("vert")
    device_total = wa_count * vert_count
    even, rest = fold_all(grid_values, row_length)
    received = fourier_all(row_length, pair_order, even, rest, device_total)
    return legendre_all(received, legendre, pair_order, wa_count, vert_count)


def solution(mesh):
    placed = (P("wa", "vert", None), P("wa"), P(), P(("wa", "vert"), None, None))
    return jax.shard_map(
        body,
        mesh=mesh,
        in_specs=placed,
        out_specs=P(("wa", "vert"), None, None, None),
        check_vma=False,
    )
```

```python
import functools
import math

import jax
import jax.numpy as jnp
from jax import lax
from jax.experimental import pallas as pl
from jax.experimental.pallas import tpu as pltpu
from jax.sharding import PartitionSpec as P

TRUNC = 1279
SUB = 256
LPAD = 5376
WAVES = TRUNC + 1
CLASS = WAVES // 4
CPAD = 384
LANE = 128
CHUNKS = 11
BLOCKS = 6
GROUPS = 8
SPAN = 4
ORDER = 5
STRIDE = 13
PART = 640


def sincos(turns):
    quarter = turns * 4.0
    near = jnp.floor(quarter + 0.5)
    f = quarter - near
    f2 = f * f
    h = math.pi / 2
    s = f * (h + f2 * (-(h**3) / 6 + f2 * (h**5 / 120 + f2 * (-(h**7) / 5040 + f2 * (h**9 / 362880)))))
    c = 1.0 + f2 * (
        -(h**2) / 2 + f2 * (h**4 / 24 + f2 * (-(h**6) / 720 + f2 * (h**8 / 40320 - f2 * (h**10 / 3628800))))
    )
    which = near - 4.0 * jnp.floor(near * 0.25)
    odd = (which == 1.0) | (which == 3.0)
    cos_out = jnp.where(odd, s, c)
    sin_out = jnp.where(odd, c, s)
    cos_out = jnp.where((which == 1.0) | (which == 2.0), -cos_out, cos_out)
    sin_out = jnp.where(which >= 2.0, -sin_out, sin_out)
    return cos_out, sin_out


def turns_of(product, n_float, inv_n):
    return (product - jnp.floor(product * inv_n) * n_float) * inv_n


def iota_f(shape, dim):
    return lax.broadcasted_iota(jnp.int32, shape, dim).astype(jnp.float32)


def fold_kernel(length_ref, grid_ref, even_ref, rest_ref, twiddle):
    def eight_rows(block, carry):
        sub = lax.broadcasted_iota(jnp.int32, (8, LANE), 0)
        n8 = jnp.zeros((8, LANE), jnp.int32)
        for e in range(8):
            n8 = jnp.where(sub == e, length_ref[block * 8 + e] // 4, n8)
        inv8 = 0.25 / n8.astype(jnp.float32)
        for j in range(CHUNKS):
            k = lax.broadcasted_iota(jnp.int32, (8, LANE), 1) + j * LANE
            c1, s1 = sincos(k.astype(jnp.float32) * inv8)
            c2 = c1 * c1 - s1 * s1
            s2 = 2.0 * c1 * s1
            c3 = c2 * c1 - s2 * s1
            s3 = s2 * c1 + c2 * s1
            inside = k < n8
            for which, v in enumerate((c1, s1, c2, s2, c3, s3)):
                v = jnp.where(inside, v, 0.0)
                for e in range(8):
                    twiddle[block * 8 + e, which : which + 1, j * LANE : (j + 1) * LANE] = v[e : e + 1]
        return carry

    lax.fori_loop(0, twiddle.shape[0] // 8, eight_rows, 0)

    lane = lax.broadcasted_iota(jnp.int32, (16, LANE), 1)
    zero = jnp.zeros((16, LANE), jnp.bfloat16)

    def one_row(t, g):
        row = t * GROUPS + g
        n = length_ref[row] // 4
        starts = []
        for part in range(4):
            start = n * part
            whole = start // LANE
            shift = start - whole * LANE
            starts.append((whole, shift, lax.rem(LANE - shift, LANE)))

        def piece(part, j):
            whole, shift, back = starts[part]
            at = pl.multiple_of((whole + j) * LANE, LANE)
            value = grid_ref[t, g, :, pl.ds(at, LANE)].astype(jnp.float32)
            return pltpu.roll(value, back, 1) if part else value

        held = [piece(part, 0) for part in range(4)]
        for j in range(CHUNKS):
            inside = lane + j * LANE < n
            quarter = []
            for part in range(4):
                value = held[part]
                following = piece(part, j + 1) if part or j + 1 < CHUNKS else None
                if part:
                    value = jnp.where(lane < LANE - starts[part][1], value, following)
                held[part] = following
                quarter.append(value)
            c1, s1, c2, s2, c3, s3 = (
                twiddle[row, which : which + 1, j * LANE : (j + 1) * LANE] for which in range(6)
            )
            qa, qb, qc, qd = quarter
            even = qa + qc
            even_other = qb + qd
            re = qa - qc
            im = qd - qb
            h2 = even - even_other
            q = j // 2
            at = (j % 2) * LANE
            even_ref[t, g, q * 16 : q * 16 + 16, at : at + LANE] = jnp.where(
                inside, even + even_other, 0.0
            ).astype(jnp.bfloat16)
            values = (
                (re * c1 + im * s1, im * c1 - re * s1),
                (h2 * c2, -(h2 * s2)),
                (re * c3 - im * s3, -(im * c3 + re * s3)),
            )
            for r, (zr, zi) in enumerate(values):
                top = (r * BLOCKS + q) * 16
                rest_ref[t, g, top : top + 16, at : at + LANE] = zr.astype(jnp.bfloat16)
                rest_ref[t, g, top : top + 16, SUB + at : SUB + at + LANE] = zi.astype(jnp.bfloat16)
        for j in range(CHUNKS, 2 * BLOCKS):
            q = j // 2
            at = (j % 2) * LANE
            even_ref[t, g, q * 16 : q * 16 + 16, at : at + LANE] = zero
            for r in range(3):
                top = (r * BLOCKS + q) * 16
                rest_ref[t, g, top : top + 16, at : at + LANE] = zero
                rest_ref[t, g, top : top + 16, SUB + at : SUB + at + LANE] = zero
        return g

    def one_group(g, carry):
        lax.fori_loop(0, SPAN, one_row, g)
        return carry

    lax.fori_loop(0, GROUPS, one_group, 0)


def fold_all(grid_values, row_length):
    row_total, field_count, points = grid_values.shape
    return pl.pallas_call(
        fold_kernel,
        in_specs=[pl.BlockSpec(memory_space=pltpu.SMEM), pl.BlockSpec(memory_space=pltpu.VMEM)],
        out_specs=[pl.BlockSpec(memory_space=pltpu.VMEM)] * 2,
        out_shape=[
            jax.ShapeDtypeStruct((SPAN, GROUPS, BLOCKS * 16, SUB), jnp.bfloat16),
            jax.ShapeDtypeStruct((SPAN, GROUPS, 3 * BLOCKS * 16, 2 * SUB), jnp.bfloat16),
        ],
        scratch_shapes=[pltpu.VMEM((row_total, 8, CHUNKS * LANE), jnp.float32)],
        compiler_params=pltpu.CompilerParams(vmem_limit_bytes=16 * 2**20),
        name="fold",
    )(row_length, grid_values.reshape(SPAN, GROUPS, field_count, points))


def fourier_kernel(
    length_ref,
    order_ref,
    even_ref,
    rest_ref,
    out_ref,
    rhs,
    small,
    onehot,
    rows,
    spread,
    sending,
    landing,
    local_sem,
    send_sem,
    recv_sem,
):
    g = pl.program_id(0)
    vert_count = lax.axis_size("vert")
    total = lax.axis_size("wa") * vert_count
    me = lax.axis_index("wa") * vert_count + lax.axis_index("vert")
    dest_rows = WAVES * GROUPS // total
    per_dest = WAVES // total

    def place(device):
        return (device // vert_count, lax.rem(device, vert_count))

    @pl.when(g == 0)
    def _():
        barrier = pltpu.get_barrier_semaphore()

        def greet(i, carry):
            other = lax.rem(me + i, total)
            pl.semaphore_signal(barrier, 1, device_id=place(other), device_id_type=pl.DeviceIdType.MESH)
            return carry

        lax.fori_loop(1, total, greet, 0)
        for c in range(per_dest):
            pair = order_ref[:, c // 2 : c // 2 + 1]
            target = TRUNC - pair if c % 2 else pair
            for r in range(4):
                wave = lax.broadcasted_iota(jnp.int32, (total, CPAD), 1) * 4 + r
                wave = jnp.where(wave < WAVES, wave, -1)
                onehot[c * total : (c + 1) * total, r * CPAD : (r + 1) * CPAD] = (
                    (wave == target).astype(jnp.float32).astype(jnp.bfloat16)
                )

    def prepare(t):
        slot = t % 2
        n = jnp.full((8, CPAD), length_ref[t * GROUPS + g] // 4, jnp.int32)
        n_float = n.astype(jnp.float32)
        inv_n = 1.0 / n_float
        u = iota_f((8, CPAD), 1)
        low = iota_f((8, CPAD), 0)
        mixed = jnp.where(low == 0.0, 8.0, jnp.where(low == 1.0, 128.0, 256.0 * (low - 1.0)))
        cb, sb = sincos(turns_of(low * u, n_float, inv_n))
        ct, st = sincos(turns_of(low * 16.0 * u, n_float, inv_n))
        cm, sm = sincos(turns_of(mixed * u, n_float, inv_n))
        small[slot, 0, :8] = ct
        small[slot, 1, :8] = st
        small[slot, 0, 16:] = cm
        small[slot, 1, 16:] = sm
        c8, s8 = small[slot, 0, 16:17, :], small[slot, 1, 16:17, :]
        c128, s128 = small[slot, 0, 17:18, :], small[slot, 1, 17:18, :]
        small[slot, 0, 8:16] = ct * c128 - st * s128
        small[slot, 1, 8:16] = st * c128 + ct * s128
        base = ((cb, sb), (cb * c8 - sb * s8, sb * c8 + cb * s8))
        for a in range(16):
            ca = small[slot, 0, a : a + 1, :]
            sa = small[slot, 1, a : a + 1, :]
            c = jnp.concatenate([x * ca - y * sa for x, y in base], axis=0)
            s = jnp.concatenate([y * ca + x * sa for x, y in base], axis=0)
            c16 = c.astype(jnp.bfloat16)
            s16 = s.astype(jnp.bfloat16)
            rhs[slot, a * 16 : a * 16 + 16, :CPAD] = c16
            rhs[slot, a * 16 : a * 16 + 16, CPAD:] = -s16
            rhs[slot, SUB + a * 16 : SUB + a * 16 + 16, :CPAD] = s16
            rhs[slot, SUB + a * 16 : SUB + a * 16 + 16, CPAD:] = c16

    paired = (g == 1) | (g == 3) | (g == 6)

    def finish(t, sums):
        slot = t % 2
        length = jnp.full((1, CPAD), length_ref[t * GROUPS + g], jnp.int32)
        scale = 1.0 / jnp.sqrt(length.astype(jnp.float32))
        column = lax.broadcasted_iota(jnp.int32, (1, CPAD), 1)
        lane_top = pl.multiple_of(jnp.where(paired, LANE, 0) + t * 32, 32)
        for r in range(4):
            part_sum, first = (sums[0], 0) if r == 0 else (sums[1], (r - 1) * 96)
            real = part_sum[first : first + 16, :CPAD]
            imag = part_sum[first : first + 16, CPAD:]
            for q in range(1, BLOCKS):
                top = first + q * 16
                pr = part_sum[top : top + 16, :CPAD]
                pi = part_sum[top : top + 16, CPAD:]
                c = small[slot, 0, 17 + q : 18 + q, :]
                s = small[slot, 1, 17 + q : 18 + q, :]
                real = real + (pr * c + pi * s)
                imag = imag + (pi * c - pr * s)
            wave = column * 4 + r
            keep = jnp.where((wave * 2 <= length - 1) & (column < CLASS), scale, 0.0)
            rows[pl.ds(lane_top, 16), r * CPAD : (r + 1) * CPAD] = (real * keep).astype(jnp.bfloat16)
            rows[pl.ds(lane_top + 16, 16), r * CPAD : (r + 1) * CPAD] = (imag * keep).astype(jnp.bfloat16)

    prepare(0)
    for t in range(SPAN):
        sums = (
            jnp.dot(even_ref[t, g], rhs[t % 2, :SUB], preferred_element_type=jnp.float32),
            jnp.dot(rest_ref[t, g], rhs[t % 2], preferred_element_type=jnp.float32),
        )
        if t + 1 < SPAN:
            prepare(t + 1)
        finish(t, sums)

    def order(count):
        for c0 in range(0, per_dest, ORDER):
            picked = lax.dot_general(
                onehot[c0 * total : (c0 + ORDER) * total, :],
                rows[: count * LANE, :],
                (((1,), (1,)), ((), ())),
                preferred_element_type=jnp.float32,
            )
            for c in range(ORDER):
                for e in range(count):
                    at = (g - count + 1 + e) * per_dest + c0 + c
                    spread[pl.ds(at, total, stride=dest_rows), :] = picked[
                        c * total : (c + 1) * total, e * LANE : (e + 1) * LANE
                    ]

    pl.when(paired)(lambda: order(2))
    pl.when((g == 4) | (g == 7))(lambda: order(1))

    @pl.when(paired | (g == 4) | (g == 7))
    def _():
        tile = (5 * (g + 1)) // 8 - 1

        def convert(d, carry):
            sending[tile, d] = spread[pl.ds(pl.multiple_of(d * dest_rows + tile * 16, 16), 16), :].astype(jnp.bfloat16)
            return carry

        lax.fori_loop(0, total, convert, 0, unroll=8)

        @pl.when(g == 1)
        def _():
            pl.semaphore_wait(pltpu.get_barrier_semaphore(), total - 1)

        pltpu.make_async_copy(sending.at[tile, me], landing.at[tile, me], local_sem.at[tile]).start()

        wa_count = lax.axis_size("wa")
        wa, vert = lax.axis_index("wa"), lax.axis_index("vert")

        def send(to_wa, to_vert):
            pltpu.make_async_remote_copy(
                sending.at[tile, to_wa * vert_count + to_vert],
                landing.at[tile, me],
                send_sem.at[tile],
                recv_sem.at[tile],
                device_id=(to_wa, to_vert),
                device_id_type=pl.DeviceIdType.MESH,
            ).start()

        for i in range(1, vert_count):
            send(wa, lax.rem(vert + i, vert_count))

        def spoke(i, carry):
            to_wa = lax.rem(wa + i * STRIDE, wa_count)
            for to_vert in range(vert_count):
                send(to_wa, to_vert)
            return carry

        lax.fori_loop(1, wa_count, spoke, 0)

    @pl.when(g == GROUPS - 1)
    def _():
        others = pl.ds(0, total - 1)
        half = lax.axis_size("wa") // 2
        lane = lax.broadcasted_iota(jnp.int32, (16, LANE), 1)
        odd32 = (lane // 32) % 2 == 1
        high64 = lane >= 64

        def regroup(tiles):
            a, b, c, d = tiles
            ab0 = jnp.where(odd32, pltpu.roll(b, 32, 1), a)
            ab1 = jnp.where(odd32, b, pltpu.roll(a, 96, 1))
            cd0 = jnp.where(odd32, pltpu.roll(d, 32, 1), c)
            cd1 = jnp.where(odd32, d, pltpu.roll(c, 96, 1))
            return (
                jnp.where(high64, pltpu.roll(cd0, 64, 1), ab0),
                jnp.where(high64, pltpu.roll(cd1, 64, 1), ab1),
                jnp.where(high64, cd0, pltpu.roll(ab0, 64, 1)),
                jnp.where(high64, cd1, pltpu.roll(ab1, 64, 1)),
            )

        def arrived(tile, carry):
            pltpu.make_async_copy(sending.at[tile, me], landing.at[tile, me], local_sem.at[tile]).wait()
            pltpu.make_async_copy(sending.at[tile, others], landing.at[tile, others], recv_sem.at[tile]).wait()

            def mirror(w, carry):
                north, south = (
                    regroup(
                        [
                            landing[tile, (side * half + w) * vert_count + v].astype(jnp.float32)
                            for v in range(SPAN)
                        ]
                    )
                    for side in range(2)
                )
                for kind in range(2):
                    for t in range(SPAN):
                        value = north[t] - south[t] if kind else north[t] + south[t]
                        top = ((w * 2 + kind) * SPAN + t) * dest_rows + tile * 16
                        spread[pl.ds(pl.multiple_of(top, 16), 16), :] = value
                return carry

            lax.fori_loop(0, half, mirror, 0)
            return carry

        lax.fori_loop(0, landing.shape[0], arrived, 0)

        def gather(w, carry):
            for kind in range(2):
                for t in range(0, SPAN, 2):
                    for col in range(per_dest):
                        both = [
                            spread[
                                pl.ds(((w * 2 + kind) * SPAN + t + e) * dest_rows + col, GROUPS, stride=per_dest), :
                            ]
                            for e in range(2)
                        ]
                        at = ((col % 2) * 2 + kind) * LANE
                        top = pl.multiple_of(w * SPAN * GROUPS + t * GROUPS, 16)
                        out_ref[col // 2, pl.ds(top, 16), at : at + LANE] = jnp.concatenate(both, axis=0).astype(
                            jnp.bfloat16
                        )
            return carry

        lax.fori_loop(0, half, gather, 0)
        for tile in range(landing.shape[0]):
            pltpu.make_async_copy(sending.at[tile, others], landing.at[tile, others], send_sem.at[tile]).wait()


def fourier_all(row_length, pair_order, even, rest, device_total):
    lat_pairs = row_length.shape[0] * lax.axis_size("wa") // 2
    tiles = WAVES * GROUPS // device_total // 16
    return pl.pallas_call(
        fourier_kernel,
        grid=(GROUPS,),
        in_specs=[
            pl.BlockSpec(memory_space=pltpu.SMEM),
            pl.BlockSpec((device_total, pair_order.shape[0] // device_total), lambda g: (0, 0)),
            pl.BlockSpec(memory_space=pltpu.VMEM),
            pl.BlockSpec(memory_space=pltpu.VMEM),
        ],
        out_specs=pl.BlockSpec(memory_space=pltpu.VMEM),
        out_shape=jax.ShapeDtypeStruct((WAVES // device_total // 2, lat_pairs, 4 * LANE), jnp.bfloat16),
        scratch_shapes=[
            pltpu.VMEM((2, 2 * SUB, 2 * CPAD), jnp.bfloat16),
            pltpu.VMEM((2, 2, 24, CPAD), jnp.float32),
            pltpu.VMEM((WAVES, 4 * CPAD), jnp.bfloat16),
            pltpu.VMEM((2 * LANE, 4 * CPAD), jnp.bfloat16),
            pltpu.VMEM((WAVES * GROUPS, LANE), jnp.float32),
            pltpu.VMEM((tiles, device_total, 16, LANE), jnp.bfloat16),
            pltpu.VMEM((tiles, device_total, 16, LANE), jnp.bfloat16),
            pltpu.SemaphoreType.DMA((tiles,)),
            pltpu.SemaphoreType.DMA((tiles,)),
            pltpu.SemaphoreType.DMA((tiles,)),
        ],
        compiler_params=pltpu.CompilerParams(
            vmem_limit_bytes=34 * 2**20, collective_id=0, has_side_effects=True
        ),
        name="fourier",
    )(row_length, pair_order.reshape(device_total, -1), even, rest)


def legendre_kernel(pair_ref, operand, leg_ref, out_ref):
    slot = pl.program_id(0)
    owner = lax.axis_index("wa") * lax.axis_size("vert") + lax.axis_index("vert")
    first_count = WAVES - pair_ref[owner * pl.num_programs(0) + slot]
    columns = leg_ref.shape[1]
    whole = columns // LANE * LANE

    def choose(product, top, out_lanes):
        height = product.shape[0]
        column = lax.broadcasted_iota(jnp.int32, (height, LANE), 0) + top
        in_first = column < first_count
        degree = jnp.where(in_first, column, column - first_count)
        even = degree % 2 == 0
        s0, a0, s1, a1 = (product[:, k * LANE : (k + 1) * LANE] for k in range(4))
        chosen = jnp.where(in_first, jnp.where(even, s0, a0), jnp.where(even, s1, a1))
        turned = chosen.T
        for v in range(4):
            for i in range(2):
                at = v * 32 + i * 16
                out_ref[0, i, v * 16 : v * 16 + 16, out_lanes] = turned[at : at + 16]

    for start in range(0, whole, PART):
        product = jnp.dot(
            leg_ref[slot, start : start + PART, :], operand[slot], preferred_element_type=jnp.float32
        )
        for top in range(0, PART, LANE):
            choose(product[top : top + LANE], start + top, slice(start + top, start + top + LANE))
    last = leg_ref[slot, whole:columns, :]
    product = jnp.dot(
        jnp.broadcast_to(last, (16, last.shape[1])), operand[slot], preferred_element_type=jnp.float32
    )
    column = jnp.zeros((16, LANE), jnp.int32) + whole
    in_first = column < first_count
    degree = jnp.where(in_first, column, column - first_count)
    even = degree % 2 == 0
    s0, a0, s1, a1 = (product[:, k * LANE : (k + 1) * LANE] for k in range(4))
    chosen = jnp.where(in_first, jnp.where(even, s0, a0), jnp.where(even, s1, a1))
    turned = jnp.broadcast_to(chosen[:1], (LANE, LANE)).T
    for v in range(4):
        for i in range(2):
            at = v * 32 + i * 16
            out_ref[0, i, v * 16 : v * 16 + 16, whole:columns] = turned[at : at + 16, : columns - whole]


def legendre_all(operand, legendre, pair_order, vert_count):
    slot_count, lat_pairs, columns = legendre.shape
    field_count = 16 * vert_count
    return pl.pallas_call(
        legendre_kernel,
        grid=(slot_count,),
        in_specs=[
            pl.BlockSpec(memory_space=pltpu.SMEM),
            pl.BlockSpec(memory_space=pltpu.VMEM),
            pl.BlockSpec(memory_space=pltpu.VMEM),
        ],
        out_specs=pl.BlockSpec((1, 2, field_count, columns), lambda s: (s, 0, 0, 0)),
        out_shape=jax.ShapeDtypeStruct((slot_count, 2, field_count, columns), jnp.float32),
        compiler_params=pltpu.CompilerParams(vmem_limit_bytes=24 * 2**20),
        name="legendre",
    )(pair_order, operand, jnp.swapaxes(legendre, 1, 2))


def body(grid_values, row_length, pair_order, legendre):
    wa_count = lax.axis_size("wa")
    vert_count = lax.axis_size("vert")
    device_total = wa_count * vert_count
    even, rest = fold_all(grid_values, row_length)
    operand = fourier_all(row_length, pair_order, even, rest, device_total)
    return legendre_all(operand, legendre, pair_order, vert_count)


def solution(mesh):
    placed = (P("wa", "vert", None), P("wa"), P(), P(("wa", "vert"), None, None))
    return jax.shard_map(
        body,
        mesh=mesh,
        in_specs=placed,
        out_specs=P(("wa", "vert"), None, None, None),
        check_vma=False,
    )
```

```python
import functools
import math

import jax
import jax.numpy as jnp
from jax import lax
from jax.experimental import pallas as pl
from jax.experimental.pallas import tpu as pltpu
from jax.sharding import PartitionSpec as P

TRUNC = 1279
SUB = 256
LPAD = 5376
WAVES = TRUNC + 1
CLASS = WAVES // 4
CPAD = 384
LANE = 128
CHUNKS = 11
BLOCKS = 6
GROUPS = 8
SPAN = 4
ORDER = 5
STRIDE = 13
PART = 640


def sincos(turns):
    quarter = turns * 4.0
    near = jnp.floor(quarter + 0.5)
    f = quarter - near
    f2 = f * f
    h = math.pi / 2
    s = f * (h + f2 * (-(h**3) / 6 + f2 * (h**5 / 120 + f2 * (-(h**7) / 5040 + f2 * (h**9 / 362880)))))
    c = 1.0 + f2 * (
        -(h**2) / 2 + f2 * (h**4 / 24 + f2 * (-(h**6) / 720 + f2 * (h**8 / 40320 - f2 * (h**10 / 3628800))))
    )
    which = near - 4.0 * jnp.floor(near * 0.25)
    odd = (which == 1.0) | (which == 3.0)
    cos_out = jnp.where(odd, s, c)
    sin_out = jnp.where(odd, c, s)
    cos_out = jnp.where((which == 1.0) | (which == 2.0), -cos_out, cos_out)
    sin_out = jnp.where(which >= 2.0, -sin_out, sin_out)
    return cos_out, sin_out


def turns_of(product, n_float, inv_n):
    return (product - jnp.floor(product * inv_n) * n_float) * inv_n


def iota_f(shape, dim):
    return lax.broadcasted_iota(jnp.int32, shape, dim).astype(jnp.float32)


def fourier_kernel(
    length_ref,
    order_ref,
    grid_ref,
    out_ref,
    chunked,
    twiddle,
    even,
    rest,
    rhs,
    small,
    onehot,
    rows,
    spread,
    sending,
    landing,
    local_sem,
    send_sem,
    recv_sem,
):
    g = pl.program_id(0)
    vert_count = lax.axis_size("vert")
    total = lax.axis_size("wa") * vert_count
    me = lax.axis_index("wa") * vert_count + lax.axis_index("vert")
    dest_rows = WAVES * GROUPS // total
    per_dest = WAVES // total

    def place(device):
        return (device // vert_count, lax.rem(device, vert_count))

    @pl.when(g % 2 == 0)
    def _():
        sub = lax.broadcasted_iota(jnp.int32, (8, LANE), 0)
        n8 = jnp.zeros((8, LANE), jnp.int32)
        for e in range(8):
            n8 = jnp.where(sub == e, length_ref[(e // 2) * GROUPS + g + e % 2] // 4, n8)
        inv8 = 0.25 / n8.astype(jnp.float32)
        for j in range(CHUNKS):
            k = lax.broadcasted_iota(jnp.int32, (8, LANE), 1) + j * LANE
            c1, s1 = sincos(k.astype(jnp.float32) * inv8)
            c2 = c1 * c1 - s1 * s1
            s2 = 2.0 * c1 * s1
            c3 = c2 * c1 - s2 * s1
            s3 = s2 * c1 + c2 * s1
            inside = k < n8
            for which, v in enumerate((c1, s1, c2, s2, c3, s3)):
                v = jnp.where(inside, v, 0.0)
                for e in range(8):
                    twiddle[e, which : which + 1, j * LANE : (j + 1) * LANE] = v[e : e + 1]

    @pl.when(g == 0)
    def _():
        for slot in range(2):
            for q in range(BLOCKS):
                even[slot, q * 16 : q * 16 + 16, :] = jnp.zeros((16, SUB), jnp.bfloat16)
            for top in range(0, 3 * BLOCKS * 16, 16):
                rest[slot, top : top + 16, :] = jnp.zeros((16, 2 * SUB), jnp.bfloat16)
        barrier = pltpu.get_barrier_semaphore()

        def greet(i, carry):
            other = lax.rem(me + i, total)
            pl.semaphore_signal(barrier, 1, device_id=place(other), device_id_type=pl.DeviceIdType.MESH)
            return carry

        lax.fori_loop(1, total, greet, 0)
        for c in range(per_dest):
            pair = order_ref[:, c // 2 : c // 2 + 1]
            target = TRUNC - pair if c % 2 else pair
            for r in range(4):
                wave = lax.broadcasted_iota(jnp.int32, (total, CPAD), 1) * 4 + r
                wave = jnp.where(wave < WAVES, wave, -1)
                onehot[c * total : (c + 1) * total, r * CPAD : (r + 1) * CPAD] = (
                    (wave == target).astype(jnp.float32).astype(jnp.bfloat16)
                )

    def fold(t):
        slot = t % 2
        n = length_ref[t * GROUPS + g] // 4
        for j in range(grid_ref.shape[3] // LANE):
            chunked[slot, j] = grid_ref[t, 0, :, j * LANE : (j + 1) * LANE]
        difference = lax.broadcasted_iota(jnp.int32, (2 * LANE, LANE), 0) - lax.broadcasted_iota(
            jnp.int32, (2 * LANE, LANE), 1
        )
        quarters = [[chunked[slot, j].astype(jnp.float32) for j in range(CHUNKS)]]
        for part in range(1, 4):
            start = n * part
            whole = start // LANE
            pick = (difference == start - whole * LANE).astype(jnp.float32).astype(jnp.bfloat16)
            pieces = [chunked[slot, whole + j] for j in range(CHUNKS + 1)]
            pairs = [jnp.concatenate([pieces[j], pieces[j + 1]], axis=1) for j in range(CHUNKS)]
            moved = jnp.dot(jnp.concatenate(pairs, axis=0), pick, preferred_element_type=jnp.float32)
            quarters.append([moved[j * 16 : j * 16 + 16] for j in range(CHUNKS)])
        lane = lax.broadcasted_iota(jnp.int32, (16, LANE), 1)
        for j in range(CHUNKS):
            c1, s1, c2, s2, c3, s3 = (
                twiddle[t * 2 + g % 2, which : which + 1, j * LANE : (j + 1) * LANE] for which in range(6)
            )
            qa, qb, qc, qd = (quarters[part][j] for part in range(4))
            even_sum = qa + qc
            odd_sum = qb + qd
            re = qa - qc
            im = qd - qb
            h2 = even_sum - odd_sum
            q = j // 2
            at = (j % 2) * LANE
            even[slot, q * 16 : q * 16 + 16, at : at + LANE] = jnp.where(
                lane + j * LANE < n, even_sum + odd_sum, 0.0
            ).astype(jnp.bfloat16)
            values = (
                (re * c1 + im * s1, im * c1 - re * s1),
                (h2 * c2, -(h2 * s2)),
                (re * c3 - im * s3, -(im * c3 + re * s3)),
            )
            for r, (zr, zi) in enumerate(values):
                top = (r * BLOCKS + q) * 16
                rest[slot, top : top + 16, at : at + LANE] = zr.astype(jnp.bfloat16)
                rest[slot, top : top + 16, SUB + at : SUB + at + LANE] = zi.astype(jnp.bfloat16)

    def prepare(t):
        fold(t)
        slot = t % 2
        n = jnp.full((8, CPAD), length_ref[t * GROUPS + g] // 4, jnp.int32)
        n_float = n.astype(jnp.float32)
        inv_n = 1.0 / n_float
        u = iota_f((8, CPAD), 1)
        low = iota_f((8, CPAD), 0)
        mixed = jnp.where(low == 0.0, 8.0, jnp.where(low == 1.0, 128.0, 256.0 * (low - 1.0)))
        cb, sb = sincos(turns_of(low * u, n_float, inv_n))
        ct, st = sincos(turns_of(low * 16.0 * u, n_float, inv_n))
        cm, sm = sincos(turns_of(mixed * u, n_float, inv_n))
        small[slot, 0, :8] = ct
        small[slot, 1, :8] = st
        small[slot, 0, 16:] = cm
        small[slot, 1, 16:] = sm
        c8, s8 = small[slot, 0, 16:17, :], small[slot, 1, 16:17, :]
        c128, s128 = small[slot, 0, 17:18, :], small[slot, 1, 17:18, :]
        small[slot, 0, 8:16] = ct * c128 - st * s128
        small[slot, 1, 8:16] = st * c128 + ct * s128
        base = ((cb, sb), (cb * c8 - sb * s8, sb * c8 + cb * s8))
        for a in range(16):
            ca = small[slot, 0, a : a + 1, :]
            sa = small[slot, 1, a : a + 1, :]
            c = jnp.concatenate([x * ca - y * sa for x, y in base], axis=0)
            s = jnp.concatenate([y * ca + x * sa for x, y in base], axis=0)
            c16 = c.astype(jnp.bfloat16)
            s16 = s.astype(jnp.bfloat16)
            rhs[slot, a * 16 : a * 16 + 16, :CPAD] = c16
            rhs[slot, a * 16 : a * 16 + 16, CPAD:] = -s16
            rhs[slot, SUB + a * 16 : SUB + a * 16 + 16, :CPAD] = s16
            rhs[slot, SUB + a * 16 : SUB + a * 16 + 16, CPAD:] = c16

    paired = (g == 1) | (g == 3) | (g == 6)

    def finish(t, sums):
        slot = t % 2
        length = jnp.full((1, CPAD), length_ref[t * GROUPS + g], jnp.int32)
        scale = 1.0 / jnp.sqrt(length.astype(jnp.float32))
        column = lax.broadcasted_iota(jnp.int32, (1, CPAD), 1)
        lane_top = pl.multiple_of(jnp.where(paired, LANE, 0) + t * 32, 32)
        for r in range(4):
            part_sum, first = (sums[0], 0) if r == 0 else (sums[1], (r - 1) * 96)
            real = part_sum[first : first + 16, :CPAD]
            imag = part_sum[first : first + 16, CPAD:]
            for q in range(1, BLOCKS):
                top = first + q * 16
                pr = part_sum[top : top + 16, :CPAD]
                pi = part_sum[top : top + 16, CPAD:]
                c = small[slot, 0, 17 + q : 18 + q, :]
                s = small[slot, 1, 17 + q : 18 + q, :]
                real = real + (pr * c + pi * s)
                imag = imag + (pi * c - pr * s)
            wave = column * 4 + r
            keep = jnp.where((wave * 2 <= length - 1) & (column < CLASS), scale, 0.0)
            rows[pl.ds(lane_top, 16), r * CPAD : (r + 1) * CPAD] = (real * keep).astype(jnp.bfloat16)
            rows[pl.ds(lane_top + 16, 16), r * CPAD : (r + 1) * CPAD] = (imag * keep).astype(jnp.bfloat16)

    prepare(0)
    for t in range(SPAN):
        sums = (
            jnp.dot(even[t % 2], rhs[t % 2, :SUB], preferred_element_type=jnp.float32),
            jnp.dot(rest[t % 2], rhs[t % 2], preferred_element_type=jnp.float32),
        )
        if t + 1 < SPAN:
            prepare(t + 1)
        finish(t, sums)

    def order(count):
        for c0 in range(0, per_dest, ORDER):
            picked = lax.dot_general(
                onehot[c0 * total : (c0 + ORDER) * total, :],
                rows[: count * LANE, :],
                (((1,), (1,)), ((), ())),
                preferred_element_type=jnp.float32,
            )
            for c in range(ORDER):
                for e in range(count):
                    at = (g - count + 1 + e) * per_dest + c0 + c
                    spread[pl.ds(at, total, stride=dest_rows), :] = picked[
                        c * total : (c + 1) * total, e * LANE : (e + 1) * LANE
                    ]

    pl.when(paired)(lambda: order(2))
    pl.when((g == 4) | (g == 7))(lambda: order(1))

    @pl.when(paired | (g == 4) | (g == 7))
    def _():
        tile = (5 * (g + 1)) // 8 - 1

        def convert(d, carry):
            sending[tile, d] = spread[pl.ds(pl.multiple_of(d * dest_rows + tile * 16, 16), 16), :].astype(jnp.bfloat16)
            return carry

        lax.fori_loop(0, total, convert, 0, unroll=8)

        @pl.when(g == 1)
        def _():
            pl.semaphore_wait(pltpu.get_barrier_semaphore(), total - 1)

        pltpu.make_async_copy(sending.at[tile, me], landing.at[tile, me], local_sem.at[tile]).start()

        wa_count = lax.axis_size("wa")
        wa, vert = lax.axis_index("wa"), lax.axis_index("vert")

        def send(to_wa, to_vert):
            pltpu.make_async_remote_copy(
                sending.at[tile, to_wa * vert_count + to_vert],
                landing.at[tile, me],
                send_sem.at[tile],
                recv_sem.at[tile],
                device_id=(to_wa, to_vert),
                device_id_type=pl.DeviceIdType.MESH,
            ).start()

        for i in range(1, vert_count):
            send(wa, lax.rem(vert + i, vert_count))

        def spoke(i, carry):
            to_wa = lax.rem(wa + i * STRIDE, wa_count)
            for to_vert in range(vert_count):
                send(to_wa, to_vert)
            return carry

        lax.fori_loop(1, wa_count, spoke, 0)

    @pl.when(g == GROUPS - 1)
    def _():
        others = pl.ds(0, total - 1)
        half = lax.axis_size("wa") // 2
        lane = lax.broadcasted_iota(jnp.int32, (16, LANE), 1)
        odd32 = (lane // 32) % 2 == 1
        high64 = lane >= 64

        def regroup(tiles):
            a, b, c, d = tiles
            ab0 = jnp.where(odd32, pltpu.roll(b, 32, 1), a)
            ab1 = jnp.where(odd32, b, pltpu.roll(a, 96, 1))
            cd0 = jnp.where(odd32, pltpu.roll(d, 32, 1), c)
            cd1 = jnp.where(odd32, d, pltpu.roll(c, 96, 1))
            return (
                jnp.where(high64, pltpu.roll(cd0, 64, 1), ab0),
                jnp.where(high64, pltpu.roll(cd1, 64, 1), ab1),
                jnp.where(high64, cd0, pltpu.roll(ab0, 64, 1)),
                jnp.where(high64, cd1, pltpu.roll(ab1, 64, 1)),
            )

        def arrived(tile, carry):
            pltpu.make_async_copy(sending.at[tile, me], landing.at[tile, me], local_sem.at[tile]).wait()
            pltpu.make_async_copy(sending.at[tile, others], landing.at[tile, others], recv_sem.at[tile]).wait()

            def mirror(w, carry):
                north, south = (
                    regroup(
                        [
                            landing[tile, (side * half + w) * vert_count + v].astype(jnp.float32)
                            for v in range(SPAN)
                        ]
                    )
                    for side in range(2)
                )
                for kind in range(2):
                    for t in range(SPAN):
                        value = north[t] - south[t] if kind else north[t] + south[t]
                        top = ((w * 2 + kind) * SPAN + t) * dest_rows + tile * 16
                        spread[pl.ds(pl.multiple_of(top, 16), 16), :] = value
                return carry

            lax.fori_loop(0, half, mirror, 0, unroll=4)
            return carry

        lax.fori_loop(0, landing.shape[0], arrived, 0)

        def gather(w, carry):
            for kind in range(2):
                for t in range(0, SPAN, 2):
                    for col in range(per_dest):
                        both = [
                            spread[
                                pl.ds(((w * 2 + kind) * SPAN + t + e) * dest_rows + col, GROUPS, stride=per_dest), :
                            ]
                            for e in range(2)
                        ]
                        at = ((col % 2) * 2 + kind) * LANE
                        top = pl.multiple_of(w * SPAN * GROUPS + t * GROUPS, 16)
                        out_ref[col // 2, pl.ds(top, 16), at : at + LANE] = jnp.concatenate(both, axis=0).astype(
                            jnp.bfloat16
                        )
            return carry

        lax.fori_loop(0, half, gather, 0)
        for tile in range(landing.shape[0]):
            pltpu.make_async_copy(sending.at[tile, others], landing.at[tile, others], send_sem.at[tile]).wait()


def fourier_all(row_length, pair_order, grid_values, device_total):
    row_total, field_count, points = grid_values.shape
    lat_pairs = row_length.shape[0] * lax.axis_size("wa") // 2
    tiles = WAVES * GROUPS // device_total // 16
    return pl.pallas_call(
        fourier_kernel,
        grid=(GROUPS,),
        in_specs=[
            pl.BlockSpec(memory_space=pltpu.SMEM),
            pl.BlockSpec((device_total, pair_order.shape[0] // device_total), lambda g: (0, 0)),
            pl.BlockSpec((SPAN, 1, field_count, points), lambda g: (0, g, 0, 0)),
        ],
        out_specs=pl.BlockSpec(memory_space=pltpu.VMEM),
        out_shape=jax.ShapeDtypeStruct((WAVES // device_total // 2, lat_pairs, 4 * LANE), jnp.bfloat16),
        scratch_shapes=[
            pltpu.VMEM((2, points // LANE, 16, LANE), jnp.bfloat16),
            pltpu.VMEM((8, 8, CHUNKS * LANE), jnp.float32),
            pltpu.VMEM((2, BLOCKS * 16, SUB), jnp.bfloat16),
            pltpu.VMEM((2, 3 * BLOCKS * 16, 2 * SUB), jnp.bfloat16),
            pltpu.VMEM((2, 2 * SUB, 2 * CPAD), jnp.bfloat16),
            pltpu.VMEM((2, 2, 24, CPAD), jnp.float32),
            pltpu.VMEM((WAVES, 4 * CPAD), jnp.bfloat16),
            pltpu.VMEM((2 * LANE, 4 * CPAD), jnp.bfloat16),
            pltpu.VMEM((WAVES * GROUPS, LANE), jnp.float32),
            pltpu.VMEM((tiles, device_total, 16, LANE), jnp.bfloat16),
            pltpu.VMEM((tiles, device_total, 16, LANE), jnp.bfloat16),
            pltpu.SemaphoreType.DMA((tiles,)),
            pltpu.SemaphoreType.DMA((tiles,)),
            pltpu.SemaphoreType.DMA((tiles,)),
        ],
        compiler_params=pltpu.CompilerParams(
            vmem_limit_bytes=48 * 2**20, collective_id=0, has_side_effects=True
        ),
        name="fourier",
    )(row_length, pair_order.reshape(device_total, -1), grid_values.reshape(SPAN, GROUPS, field_count, points))


def legendre_kernel(pair_ref, operand, leg_ref, out_ref):
    slot = pl.program_id(0)
    owner = lax.axis_index("wa") * lax.axis_size("vert") + lax.axis_index("vert")
    first_count = WAVES - pair_ref[owner * pl.num_programs(0) + slot]
    columns = leg_ref.shape[1]
    whole = columns // LANE * LANE

    def choose(product, top, out_lanes):
        height = product.shape[0]
        column = lax.broadcasted_iota(jnp.int32, (height, LANE), 0) + top
        in_first = column < first_count
        degree = jnp.where(in_first, column, column - first_count)
        even = degree % 2 == 0
        s0, a0, s1, a1 = (product[:, k * LANE : (k + 1) * LANE] for k in range(4))
        chosen = jnp.where(in_first, jnp.where(even, s0, a0), jnp.where(even, s1, a1))
        turned = chosen.T
        for v in range(4):
            for i in range(2):
                at = v * 32 + i * 16
                out_ref[0, i, v * 16 : v * 16 + 16, out_lanes] = turned[at : at + 16]

    for start in range(0, whole, PART):
        product = jnp.dot(
            leg_ref[slot, start : start + PART, :], operand[slot], preferred_element_type=jnp.float32
        )
        for top in range(0, PART, LANE):
            choose(product[top : top + LANE], start + top, slice(start + top, start + top + LANE))
    last = leg_ref[slot, whole:columns, :]
    product = jnp.dot(
        jnp.broadcast_to(last, (16, last.shape[1])), operand[slot], preferred_element_type=jnp.float32
    )
    column = jnp.zeros((16, LANE), jnp.int32) + whole
    in_first = column < first_count
    degree = jnp.where(in_first, column, column - first_count)
    even = degree % 2 == 0
    s0, a0, s1, a1 = (product[:, k * LANE : (k + 1) * LANE] for k in range(4))
    chosen = jnp.where(in_first, jnp.where(even, s0, a0), jnp.where(even, s1, a1))
    turned = jnp.broadcast_to(chosen[:1], (LANE, LANE)).T
    for v in range(4):
        for i in range(2):
            at = v * 32 + i * 16
            out_ref[0, i, v * 16 : v * 16 + 16, whole:columns] = turned[at : at + 16, : columns - whole]


def legendre_all(operand, legendre, pair_order, vert_count):
    slot_count, lat_pairs, columns = legendre.shape
    field_count = 16 * vert_count
    return pl.pallas_call(
        legendre_kernel,
        grid=(slot_count,),
        in_specs=[
            pl.BlockSpec(memory_space=pltpu.SMEM),
            pl.BlockSpec(memory_space=pltpu.VMEM),
            pl.BlockSpec(memory_space=pltpu.VMEM),
        ],
        out_specs=pl.BlockSpec((1, 2, field_count, columns), lambda s: (s, 0, 0, 0)),
        out_shape=jax.ShapeDtypeStruct((slot_count, 2, field_count, columns), jnp.float32),
        compiler_params=pltpu.CompilerParams(vmem_limit_bytes=24 * 2**20),
        name="legendre",
    )(pair_order, operand, jnp.swapaxes(legendre, 1, 2))


def body(grid_values, row_length, pair_order, legendre):
    wa_count = lax.axis_size("wa")
    vert_count = lax.axis_size("vert")
    device_total = wa_count * vert_count
    operand = fourier_all(row_length, pair_order, grid_values, device_total)
    return legendre_all(operand, legendre, pair_order, vert_count)


def solution(mesh):
    placed = (P("wa", "vert", None), P("wa"), P(), P(("wa", "vert"), None, None))
    return jax.shard_map(
        body,
        mesh=mesh,
        in_specs=placed,
        out_specs=P(("wa", "vert"), None, None, None),
        check_vma=False,
    )
```

```python
import functools
import math

import jax
import jax.numpy as jnp
from jax import lax
from jax.experimental import pallas as pl
from jax.experimental.pallas import tpu as pltpu
from jax.sharding import PartitionSpec as P

TRUNC = 1279
SUB = 256
LPAD = 5376
WAVES = TRUNC + 1
CLASS = WAVES // 4
CPAD = 384
LANE = 128
CHUNKS = 11
BLOCKS = 6
GROUPS = 8
SPAN = 4
ORDER = 5
STRIDE = 13
PART = 640


def sincos(turns):
    quarter = turns * 4.0
    near = jnp.floor(quarter + 0.5)
    f = quarter - near
    f2 = f * f
    h = math.pi / 2
    s = f * (h + f2 * (-(h**3) / 6 + f2 * (h**5 / 120 + f2 * (-(h**7) / 5040 + f2 * (h**9 / 362880)))))
    c = 1.0 + f2 * (
        -(h**2) / 2 + f2 * (h**4 / 24 + f2 * (-(h**6) / 720 + f2 * (h**8 / 40320 - f2 * (h**10 / 3628800))))
    )
    which = near - 4.0 * jnp.floor(near * 0.25)
    odd = (which == 1.0) | (which == 3.0)
    cos_out = jnp.where(odd, s, c)
    sin_out = jnp.where(odd, c, s)
    cos_out = jnp.where((which == 1.0) | (which == 2.0), -cos_out, cos_out)
    sin_out = jnp.where(which >= 2.0, -sin_out, sin_out)
    return cos_out, sin_out


def turns_of(product, n_float, inv_n):
    return (product - jnp.floor(product * inv_n) * n_float) * inv_n


def iota_f(shape, dim):
    return lax.broadcasted_iota(jnp.int32, shape, dim).astype(jnp.float32)


def fourier_kernel(
    length_ref,
    order_ref,
    grid_ref,
    out_ref,
    chunked,
    twiddle,
    even,
    rest,
    rhs,
    small,
    onehot,
    rows,
    spread,
    sending,
    landing,
    local_sem,
    send_sem,
    recv_sem,
):
    g = pl.program_id(0)
    vert_count = lax.axis_size("vert")
    total = lax.axis_size("wa") * vert_count
    me = lax.axis_index("wa") * vert_count + lax.axis_index("vert")
    dest_rows = WAVES * GROUPS // total
    per_dest = WAVES // total

    def place(device):
        return (device // vert_count, lax.rem(device, vert_count))

    @pl.when(g % 2 == 0)
    def _():
        sub = lax.broadcasted_iota(jnp.int32, (8, LANE), 0)
        n8 = jnp.zeros((8, LANE), jnp.int32)
        for e in range(8):
            n8 = jnp.where(sub == e, length_ref[(e // 2) * GROUPS + g + e % 2] // 4, n8)
        inv8 = 0.25 / n8.astype(jnp.float32)
        for j in range(CHUNKS):
            k = lax.broadcasted_iota(jnp.int32, (8, LANE), 1) + j * LANE
            c1, s1 = sincos(k.astype(jnp.float32) * inv8)
            c2 = c1 * c1 - s1 * s1
            s2 = 2.0 * c1 * s1
            c3 = c2 * c1 - s2 * s1
            s3 = s2 * c1 + c2 * s1
            inside = k < n8
            for which, v in enumerate((c1, s1, c2, s2, c3, s3)):
                v = jnp.where(inside, v, 0.0)
                for e in range(8):
                    twiddle[e, which : which + 1, j * LANE : (j + 1) * LANE] = v[e : e + 1]

    @pl.when(g == 0)
    def _():
        for slot in range(2):
            for q in range(BLOCKS):
                even[slot, q * 16 : q * 16 + 16, :] = jnp.zeros((16, SUB), jnp.bfloat16)
            for top in range(0, 3 * BLOCKS * 16, 16):
                rest[slot, top : top + 16, :] = jnp.zeros((16, 2 * SUB), jnp.bfloat16)
        barrier = pltpu.get_barrier_semaphore()

        def greet(i, carry):
            other = lax.rem(me + i, total)
            pl.semaphore_signal(barrier, 1, device_id=place(other), device_id_type=pl.DeviceIdType.MESH)
            return carry

        lax.fori_loop(1, total, greet, 0)
        at = lax.broadcasted_iota(jnp.int32, (total, WAVES), 1)
        kind = (at >= CLASS).astype(jnp.int32) + (at >= 2 * CLASS).astype(jnp.int32) + (at >= 3 * CLASS).astype(jnp.int32)
        wave = 4 * (at - CLASS * kind) + kind
        for c in range(per_dest):
            pair = order_ref[:, c // 2 : c // 2 + 1]
            target = TRUNC - pair if c % 2 else pair
            onehot[c * total : (c + 1) * total, :] = (wave == target).astype(jnp.float32).astype(jnp.bfloat16)

    def blocks_of(t):
        return BLOCKS if t == SPAN - 1 else BLOCKS - 1

    def fold(t):
        slot = t % 2
        chunks = min(CHUNKS, 2 * blocks_of(t))
        n = length_ref[t * GROUPS + g] // 4
        for j in range(grid_ref.shape[3] // LANE):
            chunked[slot, j] = grid_ref[t, 0, :, j * LANE : (j + 1) * LANE]
        lane = lax.broadcasted_iota(jnp.int32, (16, LANE), 1)
        quarters = [[chunked[slot, j].astype(jnp.float32) for j in range(chunks)]]
        for part in range(1, 4):
            start = n * part
            whole = start // LANE
            back = LANE - (start - whole * LANE)
            pieces = [chunked[slot, whole + j].astype(jnp.float32) for j in range(chunks + 1)]
            turned = [pltpu.roll(piece, lax.rem(back, LANE), 1) for piece in pieces]
            quarters.append([jnp.where(lane < back, turned[j], turned[j + 1]) for j in range(chunks)])
        for j in range(chunks):
            c1, s1, c2, s2, c3, s3 = (
                twiddle[t * 2 + g % 2, which : which + 1, j * LANE : (j + 1) * LANE] for which in range(6)
            )
            qa, qb, qc, qd = (quarters[part][j] for part in range(4))
            even_sum = qa + qc
            odd_sum = qb + qd
            re = qa - qc
            im = qd - qb
            h2 = even_sum - odd_sum
            q = j // 2
            at = (j % 2) * LANE
            even[slot, q * 16 : q * 16 + 16, at : at + LANE] = jnp.where(
                lane + j * LANE < n, even_sum + odd_sum, 0.0
            ).astype(jnp.bfloat16)
            values = (
                (re * c1 + im * s1, im * c1 - re * s1),
                (h2 * c2, -(h2 * s2)),
                (re * c3 - im * s3, -(im * c3 + re * s3)),
            )
            for r, (zr, zi) in enumerate(values):
                top = (q * 3 + r) * 16
                rest[slot, top : top + 16, at : at + LANE] = zr.astype(jnp.bfloat16)
                rest[slot, top : top + 16, SUB + at : SUB + at + LANE] = zi.astype(jnp.bfloat16)

    def prepare(t):
        fold(t)
        slot = t % 2
        n = jnp.full((8, CPAD), length_ref[t * GROUPS + g] // 4, jnp.int32)
        n_float = n.astype(jnp.float32)
        inv_n = 1.0 / n_float
        u = iota_f((8, CPAD), 1)
        low = iota_f((8, CPAD), 0)
        mixed = jnp.where(low == 0.0, 8.0, jnp.where(low == 1.0, 128.0, 256.0 * (low - 1.0)))
        cb, sb = sincos(turns_of(low * u, n_float, inv_n))
        ct, st = sincos(turns_of(low * 16.0 * u, n_float, inv_n))
        cm, sm = sincos(turns_of(mixed * u, n_float, inv_n))
        small[slot, 0, :8] = ct
        small[slot, 1, :8] = st
        small[slot, 0, 16:] = cm
        small[slot, 1, 16:] = sm
        c8, s8 = small[slot, 0, 16:17, :], small[slot, 1, 16:17, :]
        c128, s128 = small[slot, 0, 17:18, :], small[slot, 1, 17:18, :]
        small[slot, 0, 8:16] = ct * c128 - st * s128
        small[slot, 1, 8:16] = st * c128 + ct * s128
        base = ((cb, sb), (cb * c8 - sb * s8, sb * c8 + cb * s8))
        for a in range(16):
            ca = small[slot, 0, a : a + 1, :]
            sa = small[slot, 1, a : a + 1, :]
            c = jnp.concatenate([x * ca - y * sa for x, y in base], axis=0)
            s = jnp.concatenate([y * ca + x * sa for x, y in base], axis=0)
            c16 = c.astype(jnp.bfloat16)
            s16 = s.astype(jnp.bfloat16)
            rhs[slot, a * 16 : a * 16 + 16, :CPAD] = c16
            rhs[slot, a * 16 : a * 16 + 16, CPAD:] = -s16
            rhs[slot, SUB + a * 16 : SUB + a * 16 + 16, :CPAD] = s16
            rhs[slot, SUB + a * 16 : SUB + a * 16 + 16, CPAD:] = c16

    paired = (g == 1) | (g == 3) | (g == 6)

    def finish(t, sums):
        slot = t % 2
        length = jnp.full((1, CPAD), length_ref[t * GROUPS + g], jnp.int32)
        scale = 1.0 / jnp.sqrt(length.astype(jnp.float32))
        column = lax.broadcasted_iota(jnp.int32, (1, CPAD), 1)
        lane_top = pl.multiple_of(jnp.where(paired, LANE, 0) + t * 32, 32)
        left = [None, None]
        for r in range(4):
            part_sum, first, step = (sums[0], 0, 16) if r == 0 else (sums[1], (r - 1) * 16, 48)
            real = part_sum[first : first + 16, :CPAD]
            imag = part_sum[first : first + 16, CPAD:]
            for q in range(1, blocks_of(t)):
                top = first + q * step
                pr = part_sum[top : top + 16, :CPAD]
                pi = part_sum[top : top + 16, CPAD:]
                c = small[slot, 0, 17 + q : 18 + q, :]
                s = small[slot, 1, 17 + q : 18 + q, :]
                real = real + (pr * c + pi * s)
                imag = imag + (pi * c - pr * s)
            wave = column * 4 + r
            keep = jnp.where((wave * 2 <= length - 1) & (column < CLASS), scale, 0.0)
            for i, value in enumerate((real * keep, imag * keep)):
                if r % 2 == 0:
                    left[i] = value
                    continue
                right = pltpu.roll(value, CPAD - CLASS, 1)
                middle = left[i][:, 2 * LANE :] + right[:, :LANE]
                packed = jnp.concatenate([left[i][:, : 2 * LANE], middle, right[:, LANE:]], axis=1)
                at = (r // 2) * 2 * CLASS
                rows[pl.ds(lane_top + i * 16, 16), at : at + 2 * CLASS] = packed.astype(jnp.bfloat16)

    prepare(0)
    for t in range(SPAN):
        sums = (
            jnp.dot(even[t % 2, : blocks_of(t) * 16], rhs[t % 2, :SUB], preferred_element_type=jnp.float32),
            jnp.dot(rest[t % 2, : blocks_of(t) * 48], rhs[t % 2], preferred_element_type=jnp.float32),
        )
        if t + 1 < SPAN:
            prepare(t + 1)
        finish(t, sums)

    def order(count):
        for c0 in range(0, per_dest, ORDER):
            picked = lax.dot_general(
                onehot[c0 * total : (c0 + ORDER) * total, :],
                rows[: count * LANE, :],
                (((1,), (1,)), ((), ())),
                preferred_element_type=jnp.float32,
            )
            for c in range(ORDER):
                for e in range(count):
                    at = (g - count + 1 + e) * per_dest + c0 + c
                    spread[pl.ds(at, total, stride=dest_rows), :] = picked[
                        c * total : (c + 1) * total, e * LANE : (e + 1) * LANE
                    ]

    pl.when(paired)(lambda: order(2))
    pl.when((g == 4) | (g == 7))(lambda: order(1))

    @pl.when(paired | (g == 4) | (g == 7))
    def _():
        tile = (5 * (g + 1)) // 8 - 1

        def convert(d, carry):
            sending[tile, d] = spread[pl.ds(pl.multiple_of(d * dest_rows + tile * 16, 16), 16), :].astype(jnp.bfloat16)
            return carry

        lax.fori_loop(0, total, convert, 0, unroll=8)

        @pl.when(g == 1)
        def _():
            pl.semaphore_wait(pltpu.get_barrier_semaphore(), total - 1)

        pltpu.make_async_copy(sending.at[tile, me], landing.at[tile, me], local_sem.at[tile]).start()

        wa_count = lax.axis_size("wa")
        wa, vert = lax.axis_index("wa"), lax.axis_index("vert")

        def send(to_wa, to_vert):
            pltpu.make_async_remote_copy(
                sending.at[tile, to_wa * vert_count + to_vert],
                landing.at[tile, me],
                send_sem.at[tile],
                recv_sem.at[tile],
                device_id=(to_wa, to_vert),
                device_id_type=pl.DeviceIdType.MESH,
            ).start()

        for i in range(1, vert_count):
            send(wa, lax.rem(vert + i, vert_count))

        def spoke(i, carry):
            to_wa = lax.rem(wa + i * STRIDE, wa_count)
            for to_vert in range(vert_count):
                send(to_wa, to_vert)
            return carry

        lax.fori_loop(1, wa_count, spoke, 0)

    @pl.when(g == GROUPS - 1)
    def _():
        others = pl.ds(0, total - 1)
        half = lax.axis_size("wa") // 2
        lane = lax.broadcasted_iota(jnp.int32, (16, LANE), 1)
        odd32 = (lane // 32) % 2 == 1
        high64 = lane >= 64

        def regroup(tiles):
            a, b, c, d = tiles
            ab0 = jnp.where(odd32, pltpu.roll(b, 32, 1), a)
            ab1 = jnp.where(odd32, b, pltpu.roll(a, 96, 1))
            cd0 = jnp.where(odd32, pltpu.roll(d, 32, 1), c)
            cd1 = jnp.where(odd32, d, pltpu.roll(c, 96, 1))
            return (
                jnp.where(high64, pltpu.roll(cd0, 64, 1), ab0),
                jnp.where(high64, pltpu.roll(cd1, 64, 1), ab1),
                jnp.where(high64, cd0, pltpu.roll(ab0, 64, 1)),
                jnp.where(high64, cd1, pltpu.roll(ab1, 64, 1)),
            )

        def arrived(tile, carry):
            pltpu.make_async_copy(sending.at[tile, me], landing.at[tile, me], local_sem.at[tile]).wait()
            pltpu.make_async_copy(sending.at[tile, others], landing.at[tile, others], recv_sem.at[tile]).wait()

            def mirror(w, carry):
                north, south = (
                    regroup(
                        [
                            landing[tile, (side * half + w) * vert_count + v].astype(jnp.float32)
                            for v in range(SPAN)
                        ]
                    )
                    for side in range(2)
                )
                for kind in range(2):
                    for t in range(SPAN):
                        value = north[t] - south[t] if kind else north[t] + south[t]
                        top = ((w * 2 + kind) * SPAN + t) * dest_rows + tile * 16
                        spread[pl.ds(pl.multiple_of(top, 16), 16), :] = value
                return carry

            lax.fori_loop(0, half, mirror, 0, unroll=4)
            return carry

        lax.fori_loop(0, landing.shape[0], arrived, 0)

        def gather(w, carry):
            for kind in range(2):
                for t in range(0, SPAN, 2):
                    for col in range(per_dest):
                        both = [
                            spread[
                                pl.ds(((w * 2 + kind) * SPAN + t + e) * dest_rows + col, GROUPS, stride=per_dest), :
                            ]
                            for e in range(2)
                        ]
                        at = ((col % 2) * 2 + kind) * LANE
                        top = pl.multiple_of(w * SPAN * GROUPS + t * GROUPS, 16)
                        out_ref[col // 2, pl.ds(top, 16), at : at + LANE] = jnp.concatenate(both, axis=0).astype(
                            jnp.bfloat16
                        )
            return carry

        lax.fori_loop(0, half, gather, 0)
        for tile in range(landing.shape[0]):
            pltpu.make_async_copy(sending.at[tile, others], landing.at[tile, others], send_sem.at[tile]).wait()


def fourier_all(row_length, pair_order, grid_values, device_total):
    row_total, field_count, points = grid_values.shape
    lat_pairs = row_length.shape[0] * lax.axis_size("wa") // 2
    tiles = WAVES * GROUPS // device_total // 16
    return pl.pallas_call(
        fourier_kernel,
        grid=(GROUPS,),
        in_specs=[
            pl.BlockSpec(memory_space=pltpu.SMEM),
            pl.BlockSpec((device_total, pair_order.shape[0] // device_total), lambda g: (0, 0)),
            pl.BlockSpec((SPAN, 1, field_count, points), lambda g: (0, g, 0, 0)),
        ],
        out_specs=pl.BlockSpec(memory_space=pltpu.VMEM),
        out_shape=jax.ShapeDtypeStruct((WAVES // device_total // 2, lat_pairs, 4 * LANE), jnp.bfloat16),
        scratch_shapes=[
            pltpu.VMEM((2, points // LANE, 16, LANE), jnp.bfloat16),
            pltpu.VMEM((8, 8, CHUNKS * LANE), jnp.float32),
            pltpu.VMEM((2, BLOCKS * 16, SUB), jnp.bfloat16),
            pltpu.VMEM((2, 3 * BLOCKS * 16, 2 * SUB), jnp.bfloat16),
            pltpu.VMEM((2, 2 * SUB, 2 * CPAD), jnp.bfloat16),
            pltpu.VMEM((2, 2, 24, CPAD), jnp.float32),
            pltpu.VMEM((WAVES, WAVES), jnp.bfloat16),
            pltpu.VMEM((2 * LANE, WAVES), jnp.bfloat16),
            pltpu.VMEM((WAVES * GROUPS, LANE), jnp.float32),
            pltpu.VMEM((tiles, device_total, 16, LANE), jnp.bfloat16),
            pltpu.VMEM((tiles, device_total, 16, LANE), jnp.bfloat16),
            pltpu.SemaphoreType.DMA((tiles,)),
            pltpu.SemaphoreType.DMA((tiles,)),
            pltpu.SemaphoreType.DMA((tiles,)),
        ],
        compiler_params=pltpu.CompilerParams(
            vmem_limit_bytes=48 * 2**20, collective_id=0, has_side_effects=True
        ),
        name="fourier",
    )(row_length, pair_order.reshape(device_total, -1), grid_values.reshape(SPAN, GROUPS, field_count, points))


def legendre_kernel(pair_ref, operand, leg_ref, out_ref):
    slot = pl.program_id(0)
    owner = lax.axis_index("wa") * lax.axis_size("vert") + lax.axis_index("vert")
    first_count = WAVES - pair_ref[owner * pl.num_programs(0) + slot]
    columns = leg_ref.shape[1]
    whole = columns // LANE * LANE

    def choose(product, top, out_lanes):
        height = product.shape[0]
        column = lax.broadcasted_iota(jnp.int32, (height, LANE), 0) + top
        in_first = column < first_count
        degree = jnp.where(in_first, column, column - first_count)
        even = degree % 2 == 0
        s0, a0, s1, a1 = (product[:, k * LANE : (k + 1) * LANE] for k in range(4))
        chosen = jnp.where(in_first, jnp.where(even, s0, a0), jnp.where(even, s1, a1))
        turned = chosen.T
        for v in range(4):
            for i in range(2):
                at = v * 32 + i * 16
                out_ref[0, i, v * 16 : v * 16 + 16, out_lanes] = turned[at : at + 16]

    for start in range(0, whole, PART):
        product = jnp.dot(
            leg_ref[slot, start : start + PART, :], operand[slot], preferred_element_type=jnp.float32
        )
        for top in range(0, PART, LANE):
            choose(product[top : top + LANE], start + top, slice(start + top, start + top + LANE))
    last = leg_ref[slot, whole:columns, :]
    product = jnp.dot(
        jnp.broadcast_to(last, (16, last.shape[1])), operand[slot], preferred_element_type=jnp.float32
    )
    column = jnp.zeros((16, LANE), jnp.int32) + whole
    in_first = column < first_count
    degree = jnp.where(in_first, column, column - first_count)
    even = degree % 2 == 0
    s0, a0, s1, a1 = (product[:, k * LANE : (k + 1) * LANE] for k in range(4))
    chosen = jnp.where(in_first, jnp.where(even, s0, a0), jnp.where(even, s1, a1))
    turned = jnp.broadcast_to(chosen[:1], (LANE, LANE)).T
    for v in range(4):
        for i in range(2):
            at = v * 32 + i * 16
            out_ref[0, i, v * 16 : v * 16 + 16, whole:columns] = turned[at : at + 16, : columns - whole]


def legendre_all(operand, legendre, pair_order, vert_count):
    slot_count, lat_pairs, columns = legendre.shape
    field_count = 16 * vert_count
    return pl.pallas_call(
        legendre_kernel,
        grid=(slot_count,),
        in_specs=[
            pl.BlockSpec(memory_space=pltpu.SMEM),
            pl.BlockSpec(memory_space=pltpu.VMEM),
            pl.BlockSpec(memory_space=pltpu.VMEM),
        ],
        out_specs=pl.BlockSpec((1, 2, field_count, columns), lambda s: (s, 0, 0, 0)),
        out_shape=jax.ShapeDtypeStruct((slot_count, 2, field_count, columns), jnp.float32),
        compiler_params=pltpu.CompilerParams(vmem_limit_bytes=24 * 2**20),
        name="legendre",
    )(pair_order, operand, jnp.swapaxes(legendre, 1, 2))


def body(grid_values, row_length, pair_order, legendre):
    wa_count = lax.axis_size("wa")
    vert_count = lax.axis_size("vert")
    device_total = wa_count * vert_count
    operand = fourier_all(row_length, pair_order, grid_values, device_total)
    return legendre_all(operand, legendre, pair_order, vert_count)


def solution(mesh):
    placed = (P("wa", "vert", None), P("wa"), P(), P(("wa", "vert"), None, None))
    return jax.shard_map(
        body,
        mesh=mesh,
        in_specs=placed,
        out_specs=P(("wa", "vert"), None, None, None),
        check_vma=False,
    )
```

```python
import functools
import math

import jax
import jax.numpy as jnp
from jax import lax
from jax.experimental import pallas as pl
from jax.experimental.pallas import tpu as pltpu
from jax.sharding import PartitionSpec as P

TRUNC = 1279
SUB = 256
LPAD = 5376
WAVES = TRUNC + 1
CLASS = WAVES // 4
CPAD = 384
LANE = 128
CHUNKS = 11
BLOCKS = 6
GROUPS = 8
SPAN = 4
ORDER = 5
STRIDE = 13
PART = 256


def sincos(turns):
    quarter = turns * 4.0
    near = jnp.floor(quarter + 0.5)
    f = quarter - near
    f2 = f * f
    h = math.pi / 2
    s = f * (h + f2 * (-(h**3) / 6 + f2 * (h**5 / 120 + f2 * (-(h**7) / 5040 + f2 * (h**9 / 362880)))))
    c = 1.0 + f2 * (
        -(h**2) / 2 + f2 * (h**4 / 24 + f2 * (-(h**6) / 720 + f2 * (h**8 / 40320 - f2 * (h**10 / 3628800))))
    )
    which = near - 4.0 * jnp.floor(near * 0.25)
    odd = (which == 1.0) | (which == 3.0)
    cos_out = jnp.where(odd, s, c)
    sin_out = jnp.where(odd, c, s)
    cos_out = jnp.where((which == 1.0) | (which == 2.0), -cos_out, cos_out)
    sin_out = jnp.where(which >= 2.0, -sin_out, sin_out)
    return cos_out, sin_out


def turns_of(product, n_float, inv_n):
    return (product - jnp.floor(product * inv_n) * n_float) * inv_n


def iota_f(shape, dim):
    return lax.broadcasted_iota(jnp.int32, shape, dim).astype(jnp.float32)


def fourier_kernel(
    length_ref,
    order_ref,
    grid_ref,
    out_ref,
    chunked,
    twiddle,
    even,
    rest,
    rhs,
    small,
    onehot,
    rows,
    spread,
    sending,
    landing,
    local_sem,
    send_sem,
    recv_sem,
):
    g = pl.program_id(0)
    vert_count = lax.axis_size("vert")
    total = lax.axis_size("wa") * vert_count
    me = lax.axis_index("wa") * vert_count + lax.axis_index("vert")
    dest_rows = WAVES * GROUPS // total
    per_dest = WAVES // total

    @pl.when(g % 2 == 0)
    def _():
        sub = lax.broadcasted_iota(jnp.int32, (8, LANE), 0)
        n8 = jnp.zeros((8, LANE), jnp.int32)
        for e in range(8):
            n8 = jnp.where(sub == e, length_ref[(e // 2) * GROUPS + g + e % 2] // 4, n8)
        inv8 = 0.25 / n8.astype(jnp.float32)
        for j in range(CHUNKS):
            k = lax.broadcasted_iota(jnp.int32, (8, LANE), 1) + j * LANE
            c1, s1 = sincos(k.astype(jnp.float32) * inv8)
            c2 = c1 * c1 - s1 * s1
            s2 = 2.0 * c1 * s1
            c3 = c2 * c1 - s2 * s1
            s3 = s2 * c1 + c2 * s1
            inside = k < n8
            for which, v in enumerate((c1, s1, c2, s2, c3, s3)):
                v = jnp.where(inside, v, 0.0)
                for e in range(8):
                    twiddle[e, which : which + 1, j * LANE : (j + 1) * LANE] = v[e : e + 1]

    @pl.when(g == 0)
    def _():
        last = BLOCKS - 1
        even[1, last * 16 :, LANE:] = jnp.zeros((16, LANE), jnp.bfloat16)
        for side in range(2):
            rest[1, last * 48 :, side * SUB + LANE : (side + 1) * SUB] = jnp.zeros((48, LANE), jnp.bfloat16)
        wa_count = lax.axis_size("wa")
        wa, vert = lax.axis_index("wa"), lax.axis_index("vert")

        def signal(to_wa, to_vert):
            pl.semaphore_signal(
                pltpu.get_barrier_semaphore(), 1, device_id=(to_wa, to_vert), device_id_type=pl.DeviceIdType.MESH
            )

        for i in range(1, vert_count):
            signal(wa, lax.rem(vert + i, vert_count))

        def greet(i, carry):
            to_wa = lax.rem(wa + i, wa_count)
            for to_vert in range(vert_count):
                signal(to_wa, to_vert)
            return carry

        lax.fori_loop(1, wa_count, greet, 0)
        at = lax.broadcasted_iota(jnp.int32, (total, WAVES), 1)
        kind = (at >= CLASS).astype(jnp.int32) + (at >= 2 * CLASS).astype(jnp.int32) + (at >= 3 * CLASS).astype(jnp.int32)
        wave = 4 * (at - CLASS * kind) + kind
        for c in range(per_dest):
            pair = order_ref[:, c // 2 : c // 2 + 1]
            target = TRUNC - pair if c % 2 else pair
            onehot[c * total : (c + 1) * total, :] = (wave == target).astype(jnp.float32).astype(jnp.bfloat16)

    def blocks_of(t):
        return BLOCKS if t == SPAN - 1 else BLOCKS - 1

    def fold(t):
        slot = t % 2
        chunks = min(CHUNKS, 2 * blocks_of(t))
        n = length_ref[t * GROUPS + g] // 4
        for j in range(grid_ref.shape[3] // LANE):
            chunked[slot, j] = grid_ref[t, 0, :, j * LANE : (j + 1) * LANE]
        lane = lax.broadcasted_iota(jnp.int32, (16, LANE), 1)
        quarters = [[chunked[slot, j].astype(jnp.float32) for j in range(chunks)]]
        for part in range(1, 4):
            start = n * part
            whole = start // LANE
            back = LANE - (start - whole * LANE)
            pieces = [chunked[slot, whole + j].astype(jnp.float32) for j in range(chunks + 1)]
            turned = [pltpu.roll(piece, lax.rem(back, LANE), 1) for piece in pieces]
            quarters.append([jnp.where(lane < back, turned[j], turned[j + 1]) for j in range(chunks)])
        for j in range(chunks):
            c1, s1, c2, s2, c3, s3 = (
                twiddle[t * 2 + g % 2, which : which + 1, j * LANE : (j + 1) * LANE] for which in range(6)
            )
            qa, qb, qc, qd = (quarters[part][j] for part in range(4))
            even_sum = qa + qc
            odd_sum = qb + qd
            re = qa - qc
            im = qd - qb
            h2 = even_sum - odd_sum
            q = j // 2
            at = (j % 2) * LANE
            even[slot, q * 16 : q * 16 + 16, at : at + LANE] = jnp.where(
                lane + j * LANE < n, even_sum + odd_sum, 0.0
            ).astype(jnp.bfloat16)
            values = (
                (re * c1 + im * s1, im * c1 - re * s1),
                (h2 * c2, -(h2 * s2)),
                (re * c3 - im * s3, -(im * c3 + re * s3)),
            )
            for r, (zr, zi) in enumerate(values):
                top = (q * 3 + r) * 16
                rest[slot, top : top + 16, at : at + LANE] = zr.astype(jnp.bfloat16)
                rest[slot, top : top + 16, SUB + at : SUB + at + LANE] = zi.astype(jnp.bfloat16)

    def prepare(t):
        fold(t)
        slot = t % 2
        n = jnp.full((8, CPAD), length_ref[t * GROUPS + g] // 4, jnp.int32)
        n_float = n.astype(jnp.float32)
        inv_n = 1.0 / n_float
        u = iota_f((8, CPAD), 1)
        low = iota_f((8, CPAD), 0)
        mixed = jnp.where(low == 0.0, 8.0, jnp.where(low == 1.0, 128.0, 256.0 * (low - 1.0)))
        cb, sb = sincos(turns_of(low * u, n_float, inv_n))
        ct, st = sincos(turns_of(low * 16.0 * u, n_float, inv_n))
        cm, sm = sincos(turns_of(mixed * u, n_float, inv_n))
        small[slot, 0, :8] = ct
        small[slot, 1, :8] = st
        small[slot, 0, 16:] = cm
        small[slot, 1, 16:] = sm
        c8, s8 = small[slot, 0, 16:17, :], small[slot, 1, 16:17, :]
        c128, s128 = small[slot, 0, 17:18, :], small[slot, 1, 17:18, :]
        small[slot, 0, 8:16] = ct * c128 - st * s128
        small[slot, 1, 8:16] = st * c128 + ct * s128
        base = ((cb, sb), (cb * c8 - sb * s8, sb * c8 + cb * s8))
        for a in range(16):
            ca = small[slot, 0, a : a + 1, :]
            sa = small[slot, 1, a : a + 1, :]
            c = jnp.concatenate([x * ca - y * sa for x, y in base], axis=0)
            s = jnp.concatenate([y * ca + x * sa for x, y in base], axis=0)
            c16 = c.astype(jnp.bfloat16)
            s16 = s.astype(jnp.bfloat16)
            rhs[slot, a * 16 : a * 16 + 16, :CPAD] = c16
            rhs[slot, a * 16 : a * 16 + 16, CPAD:] = -s16
            rhs[slot, SUB + a * 16 : SUB + a * 16 + 16, :CPAD] = s16
            rhs[slot, SUB + a * 16 : SUB + a * 16 + 16, CPAD:] = c16

    paired = (g == 1) | (g == 3) | (g == 6)

    def finish(t, sums):
        slot = t % 2
        length = jnp.full((1, CPAD), length_ref[t * GROUPS + g], jnp.int32)
        scale = 1.0 / jnp.sqrt(length.astype(jnp.float32))
        column = lax.broadcasted_iota(jnp.int32, (1, CPAD), 1)
        lane_top = pl.multiple_of(jnp.where(paired, LANE, 0) + t * 32, 32)
        left = [None, None]
        for r in range(4):
            part_sum, first, step = (sums[0], 0, 16) if r == 0 else (sums[1], (r - 1) * 16, 48)
            real = part_sum[first : first + 16, :CPAD]
            imag = part_sum[first : first + 16, CPAD:]
            for q in range(1, blocks_of(t)):
                top = first + q * step
                pr = part_sum[top : top + 16, :CPAD]
                pi = part_sum[top : top + 16, CPAD:]
                c = small[slot, 0, 17 + q : 18 + q, :]
                s = small[slot, 1, 17 + q : 18 + q, :]
                real = real + (pr * c + pi * s)
                imag = imag + (pi * c - pr * s)
            wave = column * 4 + r
            keep = jnp.where((wave * 2 <= length - 1) & (column < CLASS), scale, 0.0)
            for i, value in enumerate((real * keep, imag * keep)):
                if r % 2 == 0:
                    left[i] = value
                    continue
                right = pltpu.roll(value, CPAD - CLASS, 1)
                middle = left[i][:, 2 * LANE :] + right[:, :LANE]
                packed = jnp.concatenate([left[i][:, : 2 * LANE], middle, right[:, LANE:]], axis=1)
                at = (r // 2) * 2 * CLASS
                rows[pl.ds(lane_top + i * 16, 16), at : at + 2 * CLASS] = packed.astype(jnp.bfloat16)

    prepare(0)
    for t in range(SPAN):
        sums = (
            jnp.dot(even[t % 2, : blocks_of(t) * 16], rhs[t % 2, :SUB], preferred_element_type=jnp.float32),
            jnp.dot(rest[t % 2, : blocks_of(t) * 48], rhs[t % 2], preferred_element_type=jnp.float32),
        )
        if t + 1 < SPAN:
            prepare(t + 1)
        finish(t, sums)

    def order(count):
        for c0 in range(0, per_dest, ORDER):
            picked = lax.dot_general(
                onehot[c0 * total : (c0 + ORDER) * total, :],
                rows[: count * LANE, :],
                (((1,), (1,)), ((), ())),
                preferred_element_type=jnp.float32,
            )
            for c in range(ORDER):
                for e in range(count):
                    at = (g - count + 1 + e) * per_dest + c0 + c
                    spread[pl.ds(at, total, stride=dest_rows), :] = picked[
                        c * total : (c + 1) * total, e * LANE : (e + 1) * LANE
                    ]

    pl.when(paired)(lambda: order(2))
    pl.when((g == 4) | (g == 7))(lambda: order(1))

    @pl.when(paired | (g == 4) | (g == 7))
    def _():
        tile = (5 * (g + 1)) // 8 - 1

        def convert(d, carry):
            sending[tile, d] = spread[pl.ds(pl.multiple_of(d * dest_rows + tile * 16, 16), 16), :].astype(jnp.bfloat16)
            return carry

        lax.fori_loop(0, total, convert, 0, unroll=8)

        @pl.when(g == 1)
        def _():
            pl.semaphore_wait(pltpu.get_barrier_semaphore(), total - 1)

        pltpu.make_async_copy(sending.at[tile, me], landing.at[tile, me], local_sem.at[tile]).start()

        wa_count = lax.axis_size("wa")
        wa, vert = lax.axis_index("wa"), lax.axis_index("vert")

        def send(to_wa, to_vert):
            pltpu.make_async_remote_copy(
                sending.at[tile, to_wa * vert_count + to_vert],
                landing.at[tile, me],
                send_sem.at[tile],
                recv_sem.at[tile],
                device_id=(to_wa, to_vert),
                device_id_type=pl.DeviceIdType.MESH,
            ).start()

        for i in range(1, vert_count):
            send(wa, lax.rem(vert + i, vert_count))

        def spoke(i, carry):
            to_wa = lax.rem(wa + i * STRIDE, wa_count)
            for to_vert in range(vert_count):
                send(to_wa, to_vert)
            return carry

        lax.fori_loop(1, wa_count, spoke, 0)

    @pl.when(g == GROUPS - 1)
    def _():
        others = pl.ds(0, total - 1)
        half = lax.axis_size("wa") // 2
        lane = lax.broadcasted_iota(jnp.int32, (16, LANE), 1)
        odd32 = (lane // 32) % 2 == 1
        high64 = lane >= 64

        def regroup(tiles):
            a, b, c, d = tiles
            ab0 = jnp.where(odd32, pltpu.roll(b, 32, 1), a)
            ab1 = jnp.where(odd32, b, pltpu.roll(a, 96, 1))
            cd0 = jnp.where(odd32, pltpu.roll(d, 32, 1), c)
            cd1 = jnp.where(odd32, d, pltpu.roll(c, 96, 1))
            return (
                jnp.where(high64, pltpu.roll(cd0, 64, 1), ab0),
                jnp.where(high64, pltpu.roll(cd1, 64, 1), ab1),
                jnp.where(high64, cd0, pltpu.roll(ab0, 64, 1)),
                jnp.where(high64, cd1, pltpu.roll(ab1, 64, 1)),
            )

        def arrived(tile, carry):
            pltpu.make_async_copy(sending.at[tile, me], landing.at[tile, me], local_sem.at[tile]).wait()
            pltpu.make_async_copy(sending.at[tile, others], landing.at[tile, others], recv_sem.at[tile]).wait()

            def mirror(w, carry):
                north, south = (
                    regroup(
                        [
                            landing[tile, (side * half + w) * vert_count + v].astype(jnp.float32)
                            for v in range(SPAN)
                        ]
                    )
                    for side in range(2)
                )
                for kind in range(2):
                    for t in range(SPAN):
                        value = north[t] - south[t] if kind else north[t] + south[t]
                        top = ((w * 2 + kind) * SPAN + t) * dest_rows + tile * 16
                        spread[pl.ds(pl.multiple_of(top, 16), 16), :] = value
                return carry

            lax.fori_loop(0, half, mirror, 0, unroll=4)
            return carry

        lax.fori_loop(0, landing.shape[0], arrived, 0)

        def gather(w, carry):
            for kind in range(2):
                for t in range(0, SPAN, 2):
                    for col in range(per_dest):
                        both = [
                            spread[
                                pl.ds(((w * 2 + kind) * SPAN + t + e) * dest_rows + col, GROUPS, stride=per_dest), :
                            ]
                            for e in range(2)
                        ]
                        at = ((col % 2) * 2 + kind) * LANE
                        top = pl.multiple_of(w * SPAN * GROUPS + t * GROUPS, 16)
                        out_ref[col // 2, pl.ds(top, 16), at : at + LANE] = jnp.concatenate(both, axis=0).astype(
                            jnp.bfloat16
                        )
            return carry

        lax.fori_loop(0, half, gather, 0)
        for tile in range(landing.shape[0]):
            pltpu.make_async_copy(sending.at[tile, others], landing.at[tile, others], send_sem.at[tile]).wait()


def fourier_all(row_length, pair_order, grid_values, device_total):
    row_total, field_count, points = grid_values.shape
    lat_pairs = row_length.shape[0] * lax.axis_size("wa") // 2
    tiles = WAVES * GROUPS // device_total // 16
    return pl.pallas_call(
        fourier_kernel,
        grid=(GROUPS,),
        in_specs=[
            pl.BlockSpec(memory_space=pltpu.SMEM),
            pl.BlockSpec((device_total, pair_order.shape[0] // device_total), lambda g: (0, 0)),
            pl.BlockSpec((SPAN, 1, field_count, points), lambda g: (0, g, 0, 0)),
        ],
        out_specs=pl.BlockSpec(memory_space=pltpu.VMEM),
        out_shape=jax.ShapeDtypeStruct((WAVES // device_total // 2, lat_pairs, 4 * LANE), jnp.bfloat16),
        scratch_shapes=[
            pltpu.VMEM((2, points // LANE, 16, LANE), jnp.bfloat16),
            pltpu.VMEM((8, 8, CHUNKS * LANE), jnp.float32),
            pltpu.VMEM((2, BLOCKS * 16, SUB), jnp.bfloat16),
            pltpu.VMEM((2, 3 * BLOCKS * 16, 2 * SUB), jnp.bfloat16),
            pltpu.VMEM((2, 2 * SUB, 2 * CPAD), jnp.bfloat16),
            pltpu.VMEM((2, 2, 24, CPAD), jnp.float32),
            pltpu.VMEM((WAVES, WAVES), jnp.bfloat16),
            pltpu.VMEM((2 * LANE, WAVES), jnp.bfloat16),
            pltpu.VMEM((WAVES * GROUPS, LANE), jnp.float32),
            pltpu.VMEM((tiles, device_total, 16, LANE), jnp.bfloat16),
            pltpu.VMEM((tiles, device_total, 16, LANE), jnp.bfloat16),
            pltpu.SemaphoreType.DMA((tiles,)),
            pltpu.SemaphoreType.DMA((tiles,)),
            pltpu.SemaphoreType.DMA((tiles,)),
        ],
        compiler_params=pltpu.CompilerParams(
            vmem_limit_bytes=48 * 2**20, collective_id=0, has_side_effects=True
        ),
        name="fourier",
    )(row_length, pair_order.reshape(device_total, -1), grid_values.reshape(SPAN, GROUPS, field_count, points))


def legendre_kernel(pair_ref, operand, leg_ref, out_ref):
    slot = pl.program_id(0)
    owner = lax.axis_index("wa") * lax.axis_size("vert") + lax.axis_index("vert")
    first_count = WAVES - pair_ref[owner * pl.num_programs(0) + slot]
    columns = leg_ref.shape[1]
    whole = columns // LANE * LANE

    def block(top, group, base):
        product = jnp.dot(
            leg_ref[slot, pl.ds(top, PART), :],
            operand[slot, :, pl.ds(pl.multiple_of(group * 2 * LANE, 2 * LANE), 2 * LANE)],
            preferred_element_type=jnp.float32,
        )
        column = lax.broadcasted_iota(jnp.int32, (PART, LANE), 0) + (top - base)
        return jnp.where(column % 2 == 0, product[:, :LANE], product[:, LANE:]).T

    def each_field():
        return [(i, v * 16, v * 32 + i * 16) for v in range(4) for i in range(2)]

    for top in range(0, whole, PART):
        second = (top >= first_count).astype(jnp.int32)
        turned = block(top, second, second * first_count)
        for i, field, at in each_field():
            out_ref[0, i, field : field + 16, top : top + PART] = turned[at : at + 16]

    @pl.when(first_count % PART != 0)
    def _():
        top = pl.multiple_of(first_count // PART * PART, PART)
        turned = block(top, 1, first_count)
        first = lax.broadcasted_iota(jnp.int32, (16, PART), 1) + top < first_count
        for i, field, at in each_field():
            lanes = pl.ds(top, PART)
            out_ref[0, i, field : field + 16, lanes] = jnp.where(
                first, out_ref[0, i, field : field + 16, lanes], turned[at : at + 16]
            )

    last = leg_ref[slot, whole:columns, :]
    product = jnp.dot(
        jnp.broadcast_to(last, (16, last.shape[1])), operand[slot], preferred_element_type=jnp.float32
    )
    column = jnp.zeros((16, LANE), jnp.int32) + whole
    in_first = column < first_count
    degree = jnp.where(in_first, column, column - first_count)
    even = degree % 2 == 0
    s0, a0, s1, a1 = (product[:, k * LANE : (k + 1) * LANE] for k in range(4))
    chosen = jnp.where(in_first, jnp.where(even, s0, a0), jnp.where(even, s1, a1))
    turned = jnp.broadcast_to(chosen[:1], (LANE, LANE)).T
    for v in range(4):
        for i in range(2):
            at = v * 32 + i * 16
            out_ref[0, i, v * 16 : v * 16 + 16, whole:columns] = turned[at : at + 16, : columns - whole]


def legendre_all(operand, legendre, pair_order, vert_count):
    slot_count, lat_pairs, columns = legendre.shape
    field_count = 16 * vert_count
    return pl.pallas_call(
        legendre_kernel,
        grid=(slot_count,),
        in_specs=[
            pl.BlockSpec(memory_space=pltpu.SMEM),
            pl.BlockSpec(memory_space=pltpu.VMEM),
            pl.BlockSpec(memory_space=pltpu.VMEM),
        ],
        out_specs=pl.BlockSpec((1, 2, field_count, columns), lambda s: (s, 0, 0, 0)),
        out_shape=jax.ShapeDtypeStruct((slot_count, 2, field_count, columns), jnp.float32),
        compiler_params=pltpu.CompilerParams(vmem_limit_bytes=24 * 2**20),
        name="legendre",
    )(pair_order, operand, jnp.swapaxes(legendre, 1, 2))


def body(grid_values, row_length, pair_order, legendre):
    wa_count = lax.axis_size("wa")
    vert_count = lax.axis_size("vert")
    device_total = wa_count * vert_count
    operand = fourier_all(row_length, pair_order, grid_values, device_total)
    return legendre_all(operand, legendre, pair_order, vert_count)


def solution(mesh):
    placed = (P("wa", "vert", None), P("wa"), P(), P(("wa", "vert"), None, None))
    return jax.shard_map(
        body,
        mesh=mesh,
        in_specs=placed,
        out_specs=P(("wa", "vert"), None, None, None),
        check_vma=False,
    )
```

```python
import functools
import math

import jax
import jax.numpy as jnp
from jax import lax
from jax.experimental import pallas as pl
from jax.experimental.pallas import tpu as pltpu
from jax.sharding import PartitionSpec as P

TRUNC = 1279
SUB = 256
LPAD = 5376
WAVES = TRUNC + 1
CLASS = WAVES // 4
CPAD = 384
LANE = 128
CHUNKS = 11
BLOCKS = 6
GROUPS = 8
SPAN = 4
ORDER = 5
STRIDE = 13
PART = 256


def sincos(turns):
    quarter = turns * 4.0
    near = jnp.floor(quarter + 0.5)
    f = quarter - near
    f2 = f * f
    h = math.pi / 2
    s = f * (h + f2 * (-(h**3) / 6 + f2 * (h**5 / 120 + f2 * (-(h**7) / 5040 + f2 * (h**9 / 362880)))))
    c = 1.0 + f2 * (
        -(h**2) / 2 + f2 * (h**4 / 24 + f2 * (-(h**6) / 720 + f2 * (h**8 / 40320 - f2 * (h**10 / 3628800))))
    )
    which = near - 4.0 * jnp.floor(near * 0.25)
    odd = (which == 1.0) | (which == 3.0)
    cos_out = jnp.where(odd, s, c)
    sin_out = jnp.where(odd, c, s)
    cos_out = jnp.where((which == 1.0) | (which == 2.0), -cos_out, cos_out)
    sin_out = jnp.where(which >= 2.0, -sin_out, sin_out)
    return cos_out, sin_out


def turns_of(product, n_float, inv_n):
    return (product - jnp.floor(product * inv_n) * n_float) * inv_n


def iota_f(shape, dim):
    return lax.broadcasted_iota(jnp.int32, shape, dim).astype(jnp.float32)


def fourier_kernel(
    length_ref,
    order_ref,
    grid_ref,
    out_ref,
    chunked,
    twiddle,
    even,
    rest,
    rhs,
    small,
    onehot,
    rows,
    spread,
    sending,
    landing,
    local_sem,
    send_sem,
    recv_sem,
):
    g = pl.program_id(0)
    vert_count = lax.axis_size("vert")
    total = lax.axis_size("wa") * vert_count
    me = lax.axis_index("wa") * vert_count + lax.axis_index("vert")
    dest_rows = WAVES * GROUPS // total
    per_dest = WAVES // total

    @pl.when(g % 2 == 0)
    def _():
        sub = lax.broadcasted_iota(jnp.int32, (8, LANE), 0)
        n8 = jnp.zeros((8, LANE), jnp.int32)
        for e in range(8):
            n8 = jnp.where(sub == e, length_ref[(e // 2) * GROUPS + g + e % 2] // 4, n8)
        inv8 = 0.25 / n8.astype(jnp.float32)
        for j in range(CHUNKS):
            k = lax.broadcasted_iota(jnp.int32, (8, LANE), 1) + j * LANE
            c1, s1 = sincos(k.astype(jnp.float32) * inv8)
            c2 = c1 * c1 - s1 * s1
            s2 = 2.0 * c1 * s1
            c3 = c2 * c1 - s2 * s1
            s3 = s2 * c1 + c2 * s1
            inside = k < n8
            for which, v in enumerate((c1, s1, c2, s2, c3, s3)):
                v = jnp.where(inside, v, 0.0)
                for e in range(8):
                    twiddle[e, which : which + 1, j * LANE : (j + 1) * LANE] = v[e : e + 1]

    @pl.when(g == 0)
    def _():
        last = BLOCKS - 1
        even[1, last * 16 :, LANE:] = jnp.zeros((16, LANE), jnp.bfloat16)
        for side in range(2):
            rest[1, last * 48 :, side * SUB + LANE : (side + 1) * SUB] = jnp.zeros((48, LANE), jnp.bfloat16)
        wa_count = lax.axis_size("wa")
        wa, vert = lax.axis_index("wa"), lax.axis_index("vert")

        def signal(to_wa, to_vert):
            pl.semaphore_signal(
                pltpu.get_barrier_semaphore(), 1, device_id=(to_wa, to_vert), device_id_type=pl.DeviceIdType.MESH
            )

        for i in range(1, vert_count):
            signal(wa, lax.rem(vert + i, vert_count))

        def greet(i, carry):
            to_wa = lax.rem(wa + i, wa_count)
            for to_vert in range(vert_count):
                signal(to_wa, to_vert)
            return carry

        lax.fori_loop(1, wa_count, greet, 0)
        at = lax.broadcasted_iota(jnp.int32, (total, WAVES), 1)
        kind = (at >= CLASS).astype(jnp.int32) + (at >= 2 * CLASS).astype(jnp.int32) + (at >= 3 * CLASS).astype(jnp.int32)
        wave = 4 * (at - CLASS * kind) + kind
        for c in range(per_dest):
            pair = order_ref[:, c // 2 : c // 2 + 1]
            target = TRUNC - pair if c % 2 else pair
            onehot[c * total : (c + 1) * total, :] = (wave == target).astype(jnp.float32).astype(jnp.bfloat16)

    def blocks_of(t):
        return BLOCKS if t == SPAN - 1 else BLOCKS - 1

    def fold(t):
        slot = t % 2
        chunks = min(CHUNKS, 2 * blocks_of(t))
        n = length_ref[t * GROUPS + g] // 4
        for j in range(grid_ref.shape[3] // LANE):
            chunked[slot, j] = grid_ref[t, 0, :, j * LANE : (j + 1) * LANE]
        lane = lax.broadcasted_iota(jnp.int32, (16, LANE), 1)
        quarters = [[chunked[slot, j].astype(jnp.float32) for j in range(chunks)]]
        for part in range(1, 4):
            start = n * part
            whole = start // LANE
            back = LANE - (start - whole * LANE)
            pieces = [chunked[slot, whole + j].astype(jnp.float32) for j in range(chunks + 1)]
            turned = [pltpu.roll(piece, lax.rem(back, LANE), 1) for piece in pieces]
            quarters.append([jnp.where(lane < back, turned[j], turned[j + 1]) for j in range(chunks)])
        for j in range(chunks):
            c1, s1, c2, s2, c3, s3 = (
                twiddle[t * 2 + g % 2, which : which + 1, j * LANE : (j + 1) * LANE] for which in range(6)
            )
            qa, qb, qc, qd = (quarters[part][j] for part in range(4))
            even_sum = qa + qc
            odd_sum = qb + qd
            re = qa - qc
            im = qd - qb
            h2 = even_sum - odd_sum
            q = j // 2
            at = (j % 2) * LANE
            even[slot, q * 16 : q * 16 + 16, at : at + LANE] = jnp.where(
                lane + j * LANE < n, even_sum + odd_sum, 0.0
            ).astype(jnp.bfloat16)
            values = (
                (re * c1 + im * s1, im * c1 - re * s1),
                (h2 * c2, -(h2 * s2)),
                (re * c3 - im * s3, -(im * c3 + re * s3)),
            )
            for r, (zr, zi) in enumerate(values):
                top = (q * 3 + r) * 16
                rest[slot, top : top + 16, at : at + LANE] = zr.astype(jnp.bfloat16)
                rest[slot, top : top + 16, SUB + at : SUB + at + LANE] = zi.astype(jnp.bfloat16)

    def prepare(t):
        fold(t)
        slot = t % 2
        n = jnp.full((8, CPAD), length_ref[t * GROUPS + g] // 4, jnp.int32)
        n_float = n.astype(jnp.float32)
        inv_n = 1.0 / n_float
        u = iota_f((8, CPAD), 1)
        low = iota_f((8, CPAD), 0)
        mixed = jnp.where(low == 0.0, 8.0, jnp.where(low == 1.0, 128.0, 256.0 * (low - 1.0)))
        cb, sb = sincos(turns_of(low * u, n_float, inv_n))
        ct, st = sincos(turns_of(low * 16.0 * u, n_float, inv_n))
        cm, sm = sincos(turns_of(mixed * u, n_float, inv_n))
        small[slot, 0, :8] = ct
        small[slot, 1, :8] = st
        small[slot, 0, 16:] = cm
        small[slot, 1, 16:] = sm
        c8, s8 = small[slot, 0, 16:17, :], small[slot, 1, 16:17, :]
        c128, s128 = small[slot, 0, 17:18, :], small[slot, 1, 17:18, :]
        small[slot, 0, 8:16] = ct * c128 - st * s128
        small[slot, 1, 8:16] = st * c128 + ct * s128
        base = ((cb, sb), (cb * c8 - sb * s8, sb * c8 + cb * s8))
        for a in range(16):
            ca = small[slot, 0, a : a + 1, :]
            sa = small[slot, 1, a : a + 1, :]
            c = jnp.concatenate([x * ca - y * sa for x, y in base], axis=0)
            s = jnp.concatenate([y * ca + x * sa for x, y in base], axis=0)
            c16 = c.astype(jnp.bfloat16)
            s16 = s.astype(jnp.bfloat16)
            rhs[slot, a * 16 : a * 16 + 16, :CPAD] = c16
            rhs[slot, a * 16 : a * 16 + 16, CPAD:] = -s16
            rhs[slot, SUB + a * 16 : SUB + a * 16 + 16, :CPAD] = s16
            rhs[slot, SUB + a * 16 : SUB + a * 16 + 16, CPAD:] = c16

    paired = (g == 1) | (g == 3) | (g == 6)

    def finish(t, sums):
        slot = t % 2
        length = jnp.full((1, CPAD), length_ref[t * GROUPS + g], jnp.int32)
        scale = 1.0 / jnp.sqrt(length.astype(jnp.float32))
        column = lax.broadcasted_iota(jnp.int32, (1, CPAD), 1)
        lane_top = pl.multiple_of(jnp.where(paired, LANE, 0) + t * 32, 32)
        left = [None, None]
        for r in range(4):
            part_sum, first, step = (sums[0], 0, 16) if r == 0 else (sums[1], (r - 1) * 16, 48)
            real = part_sum[first : first + 16, :CPAD]
            imag = part_sum[first : first + 16, CPAD:]
            for q in range(1, blocks_of(t)):
                top = first + q * step
                pr = part_sum[top : top + 16, :CPAD]
                pi = part_sum[top : top + 16, CPAD:]
                c = small[slot, 0, 17 + q : 18 + q, :]
                s = small[slot, 1, 17 + q : 18 + q, :]
                real = real + (pr * c + pi * s)
                imag = imag + (pi * c - pr * s)
            wave = column * 4 + r
            keep = jnp.where((wave * 2 <= length - 1) & (column < CLASS), scale, 0.0)
            for i, value in enumerate((real * keep, imag * keep)):
                if r % 2 == 0:
                    left[i] = value
                    continue
                right = pltpu.roll(value, CPAD - CLASS, 1)
                middle = left[i][:, 2 * LANE :] + right[:, :LANE]
                packed = jnp.concatenate([left[i][:, : 2 * LANE], middle, right[:, LANE:]], axis=1)
                at = (r // 2) * 2 * CLASS
                rows[pl.ds(lane_top + i * 16, 16), at : at + 2 * CLASS] = packed.astype(jnp.bfloat16)

    prepare(0)
    for t in range(SPAN):
        sums = (
            jnp.dot(even[t % 2, : blocks_of(t) * 16], rhs[t % 2, :SUB], preferred_element_type=jnp.float32),
            jnp.dot(rest[t % 2, : blocks_of(t) * 48], rhs[t % 2], preferred_element_type=jnp.float32),
        )
        if t + 1 < SPAN:
            prepare(t + 1)
        finish(t, sums)

    def order(count):
        for c0 in range(0, per_dest, ORDER):
            picked = lax.dot_general(
                onehot[c0 * total : (c0 + ORDER) * total, :],
                rows[: count * LANE, :],
                (((1,), (1,)), ((), ())),
                preferred_element_type=jnp.float32,
            )
            for c in range(ORDER):
                for e in range(count):
                    at = (g - count + 1 + e) * per_dest + c0 + c
                    spread[pl.ds(at, total, stride=dest_rows), :] = picked[
                        c * total : (c + 1) * total, e * LANE : (e + 1) * LANE
                    ]

    pl.when(paired)(lambda: order(2))
    pl.when((g == 4) | (g == 7))(lambda: order(1))

    @pl.when(paired | (g == 4) | (g == 7))
    def _():
        tile = (5 * (g + 1)) // 8 - 1

        def convert(d, carry):
            sending[tile, d] = spread[pl.ds(pl.multiple_of(d * dest_rows + tile * 16, 16), 16), :].astype(jnp.bfloat16)
            return carry

        lax.fori_loop(0, total, convert, 0, unroll=8)

        @pl.when(g == 1)
        def _():
            pl.semaphore_wait(pltpu.get_barrier_semaphore(), total - 1)

        pltpu.make_async_copy(sending.at[tile, me], landing.at[tile, me], local_sem.at[tile]).start()

        wa_count = lax.axis_size("wa")
        wa, vert = lax.axis_index("wa"), lax.axis_index("vert")

        def send(to_wa, to_vert):
            pltpu.make_async_remote_copy(
                sending.at[tile, to_wa * vert_count + to_vert],
                landing.at[tile, me],
                send_sem.at[tile],
                recv_sem.at[tile],
                device_id=(to_wa, to_vert),
                device_id_type=pl.DeviceIdType.MESH,
            ).start()

        for i in range(1, vert_count):
            send(wa, lax.rem(vert + i, vert_count))

        def spoke(i, carry):
            to_wa = lax.rem(wa + i * STRIDE, wa_count)
            for to_vert in range(vert_count):
                send(to_wa, to_vert)
            return carry

        lax.fori_loop(1, wa_count, spoke, 0)

    @pl.when(g == GROUPS - 1)
    def _():
        others = pl.ds(0, total - 1)
        half = lax.axis_size("wa") // 2
        lane = lax.broadcasted_iota(jnp.int32, (16, LANE), 1)
        odd32 = (lane // 32) % 2 == 1
        high64 = lane >= 64

        def regroup(tiles):
            a, b, c, d = tiles
            ab0 = jnp.where(odd32, pltpu.roll(b, 32, 1), a)
            ab1 = jnp.where(odd32, b, pltpu.roll(a, 96, 1))
            cd0 = jnp.where(odd32, pltpu.roll(d, 32, 1), c)
            cd1 = jnp.where(odd32, d, pltpu.roll(c, 96, 1))
            return (
                jnp.where(high64, pltpu.roll(cd0, 64, 1), ab0),
                jnp.where(high64, pltpu.roll(cd1, 64, 1), ab1),
                jnp.where(high64, cd0, pltpu.roll(ab0, 64, 1)),
                jnp.where(high64, cd1, pltpu.roll(ab1, 64, 1)),
            )

        def arrived(tile, carry):
            pltpu.make_async_copy(sending.at[tile, me], landing.at[tile, me], local_sem.at[tile]).wait()
            pltpu.make_async_copy(sending.at[tile, others], landing.at[tile, others], recv_sem.at[tile]).wait()

            def mirror(w, carry):
                north, south = (
                    regroup(
                        [
                            landing[tile, (side * half + w) * vert_count + v].astype(jnp.float32)
                            for v in range(SPAN)
                        ]
                    )
                    for side in range(2)
                )
                for kind in range(2):
                    for t in range(SPAN):
                        value = north[t] - south[t] if kind else north[t] + south[t]
                        top = ((w * 2 + kind) * SPAN + t) * dest_rows + tile * 16
                        spread[pl.ds(pl.multiple_of(top, 16), 16), :] = value
                return carry

            lax.fori_loop(0, half, mirror, 0, unroll=4)
            return carry

        lax.fori_loop(0, landing.shape[0], arrived, 0)

        def gather(w, carry):
            for kind in range(2):
                for t in range(0, SPAN, 2):
                    for col in range(per_dest):
                        both = [
                            spread[
                                pl.ds(((w * 2 + kind) * SPAN + t + e) * dest_rows + col, GROUPS, stride=per_dest), :
                            ]
                            for e in range(2)
                        ]
                        at = ((col % 2) * 2 + kind) * LANE
                        top = pl.multiple_of(w * SPAN * GROUPS + t * GROUPS, 16)
                        out_ref[col // 2, pl.ds(top, 16), at : at + LANE] = jnp.concatenate(both, axis=0).astype(
                            jnp.bfloat16
                        )
            return carry

        lax.fori_loop(0, half, gather, 0)
        for tile in range(landing.shape[0]):
            pltpu.make_async_copy(sending.at[tile, others], landing.at[tile, others], send_sem.at[tile]).wait()


def fourier_all(row_length, pair_order, grid_values, device_total):
    row_total, field_count, points = grid_values.shape
    lat_pairs = row_length.shape[0] * lax.axis_size("wa") // 2
    tiles = WAVES * GROUPS // device_total // 16
    return pl.pallas_call(
        fourier_kernel,
        grid=(GROUPS,),
        in_specs=[
            pl.BlockSpec(memory_space=pltpu.SMEM),
            pl.BlockSpec((device_total, pair_order.shape[0] // device_total), lambda g: (0, 0)),
            pl.BlockSpec((SPAN, 1, field_count, points), lambda g: (0, g, 0, 0)),
        ],
        out_specs=pl.BlockSpec(memory_space=pltpu.VMEM),
        out_shape=jax.ShapeDtypeStruct((WAVES // device_total // 2, lat_pairs, 4 * LANE), jnp.bfloat16),
        scratch_shapes=[
            pltpu.VMEM((2, points // LANE, 16, LANE), jnp.bfloat16),
            pltpu.VMEM((8, 8, CHUNKS * LANE), jnp.float32),
            pltpu.VMEM((2, BLOCKS * 16, SUB), jnp.bfloat16),
            pltpu.VMEM((2, 3 * BLOCKS * 16, 2 * SUB), jnp.bfloat16),
            pltpu.VMEM((2, 2 * SUB, 2 * CPAD), jnp.bfloat16),
            pltpu.VMEM((2, 2, 24, CPAD), jnp.float32),
            pltpu.VMEM((WAVES, WAVES), jnp.bfloat16),
            pltpu.VMEM((2 * LANE, WAVES), jnp.bfloat16),
            pltpu.VMEM((WAVES * GROUPS, LANE), jnp.float32),
            pltpu.VMEM((tiles, device_total, 16, LANE), jnp.bfloat16),
            pltpu.VMEM((tiles, device_total, 16, LANE), jnp.bfloat16),
            pltpu.SemaphoreType.DMA((tiles,)),
            pltpu.SemaphoreType.DMA((tiles,)),
            pltpu.SemaphoreType.DMA((tiles,)),
        ],
        compiler_params=pltpu.CompilerParams(
            vmem_limit_bytes=48 * 2**20, collective_id=0, has_side_effects=True
        ),
        name="fourier",
    )(row_length, pair_order.reshape(device_total, -1), grid_values.reshape(SPAN, GROUPS, field_count, points))


def legendre_kernel(pair_ref, operand, leg_ref, out_ref):
    slot = pl.program_id(0)
    owner = lax.axis_index("wa") * lax.axis_size("vert") + lax.axis_index("vert")
    first_count = WAVES - pair_ref[owner * pl.num_programs(0) + slot]
    columns = leg_ref.shape[1]
    whole = columns // LANE * LANE

    def choose(product, top, out_lanes):
        height = product.shape[0]
        column = lax.broadcasted_iota(jnp.int32, (height, LANE), 0) + top
        in_first = column < first_count
        degree = jnp.where(in_first, column, column - first_count)
        even = degree % 2 == 0
        s0, a0, s1, a1 = (product[:, k * LANE : (k + 1) * LANE] for k in range(4))
        chosen = jnp.where(in_first, jnp.where(even, s0, a0), jnp.where(even, s1, a1))
        turned = chosen.T
        for v in range(4):
            for i in range(2):
                at = v * 32 + i * 16
                out_ref[0, i, v * 16 : v * 16 + 16, out_lanes] = turned[at : at + 16]

    for start in range(0, whole, PART):
        product = jnp.dot(
            leg_ref[slot, start : start + PART, :], operand[slot], preferred_element_type=jnp.float32
        )
        for top in range(0, PART, LANE):
            choose(product[top : top + LANE], start + top, slice(start + top, start + top + LANE))
    last = leg_ref[slot, whole:columns, :]
    product = jnp.dot(
        jnp.broadcast_to(last, (16, last.shape[1])), operand[slot], preferred_element_type=jnp.float32
    )
    column = jnp.zeros((16, LANE), jnp.int32) + whole
    in_first = column < first_count
    degree = jnp.where(in_first, column, column - first_count)
    even = degree % 2 == 0
    s0, a0, s1, a1 = (product[:, k * LANE : (k + 1) * LANE] for k in range(4))
    chosen = jnp.where(in_first, jnp.where(even, s0, a0), jnp.where(even, s1, a1))
    turned = jnp.broadcast_to(chosen[:1], (LANE, LANE)).T
    for v in range(4):
        for i in range(2):
            at = v * 32 + i * 16
            out_ref[0, i, v * 16 : v * 16 + 16, whole:columns] = turned[at : at + 16, : columns - whole]


def legendre_all(operand, legendre, pair_order, vert_count):
    slot_count, lat_pairs, columns = legendre.shape
    field_count = 16 * vert_count
    return pl.pallas_call(
        legendre_kernel,
        grid=(slot_count,),
        in_specs=[
            pl.BlockSpec(memory_space=pltpu.SMEM),
            pl.BlockSpec(memory_space=pltpu.VMEM),
            pl.BlockSpec(memory_space=pltpu.VMEM),
        ],
        out_specs=pl.BlockSpec((1, 2, field_count, columns), lambda s: (s, 0, 0, 0)),
        out_shape=jax.ShapeDtypeStruct((slot_count, 2, field_count, columns), jnp.float32),
        compiler_params=pltpu.CompilerParams(vmem_limit_bytes=24 * 2**20),
        name="legendre",
    )(pair_order, operand, jnp.swapaxes(legendre, 1, 2))


def body(grid_values, row_length, pair_order, legendre):
    wa_count = lax.axis_size("wa")
    vert_count = lax.axis_size("vert")
    device_total = wa_count * vert_count
    operand = fourier_all(row_length, pair_order, grid_values, device_total)
    return legendre_all(operand, legendre, pair_order, vert_count)


def solution(mesh):
    placed = (P("wa", "vert", None), P("wa"), P(), P(("wa", "vert"), None, None))
    return jax.shard_map(
        body,
        mesh=mesh,
        in_specs=placed,
        out_specs=P(("wa", "vert"), None, None, None),
        check_vma=False,
    )
```

```python
import functools
import math

import jax
import jax.numpy as jnp
from jax import lax
from jax.experimental import pallas as pl
from jax.experimental.pallas import tpu as pltpu
from jax.sharding import PartitionSpec as P

TRUNC = 1279
SUB = 256
LPAD = 5376
WAVES = TRUNC + 1
CLASS = WAVES // 4
CPAD = 384
LANE = 128
CHUNKS = 11
BLOCKS = 6
GROUPS = 8
SPAN = 4
ORDER = 5
STRIDE = 13
PART = 256


def sincos(turns):
    quarter = turns * 4.0
    near = jnp.floor(quarter + 0.5)
    f = quarter - near
    f2 = f * f
    h = math.pi / 2
    s = f * (h + f2 * (-(h**3) / 6 + f2 * (h**5 / 120 + f2 * (-(h**7) / 5040 + f2 * (h**9 / 362880)))))
    c = 1.0 + f2 * (
        -(h**2) / 2 + f2 * (h**4 / 24 + f2 * (-(h**6) / 720 + f2 * (h**8 / 40320 - f2 * (h**10 / 3628800))))
    )
    which = near - 4.0 * jnp.floor(near * 0.25)
    odd = (which == 1.0) | (which == 3.0)
    cos_out = jnp.where(odd, s, c)
    sin_out = jnp.where(odd, c, s)
    cos_out = jnp.where((which == 1.0) | (which == 2.0), -cos_out, cos_out)
    sin_out = jnp.where(which >= 2.0, -sin_out, sin_out)
    return cos_out, sin_out


def turns_of(product, n_float, inv_n):
    return (product - jnp.floor(product * inv_n) * n_float) * inv_n


def iota_f(shape, dim):
    return lax.broadcasted_iota(jnp.int32, shape, dim).astype(jnp.float32)


def fourier_kernel(
    length_ref,
    order_ref,
    grid_ref,
    out_ref,
    chunked,
    twiddle,
    even,
    rest,
    rhs,
    small,
    onehot,
    rows,
    spread,
    sending,
    landing,
    local_sem,
    send_sem,
    recv_sem,
):
    g = pl.program_id(0)
    vert_count = lax.axis_size("vert")
    total = lax.axis_size("wa") * vert_count
    me = lax.axis_index("wa") * vert_count + lax.axis_index("vert")
    dest_rows = WAVES * GROUPS // total
    per_dest = WAVES // total

    @pl.when(g % 2 == 0)
    def _():
        sub = lax.broadcasted_iota(jnp.int32, (8, LANE), 0)
        n8 = jnp.zeros((8, LANE), jnp.int32)
        for e in range(8):
            n8 = jnp.where(sub == e, length_ref[(e // 2) * GROUPS + g + e % 2] // 4, n8)
        inv8 = 0.25 / n8.astype(jnp.float32)
        for j in range(CHUNKS):
            k = lax.broadcasted_iota(jnp.int32, (8, LANE), 1) + j * LANE
            c1, s1 = sincos(k.astype(jnp.float32) * inv8)
            c2 = c1 * c1 - s1 * s1
            s2 = 2.0 * c1 * s1
            c3 = c2 * c1 - s2 * s1
            s3 = s2 * c1 + c2 * s1
            inside = k < n8
            for which, v in enumerate((c1, s1, c2, s2, c3, s3)):
                v = jnp.where(inside, v, 0.0)
                for e in range(8):
                    twiddle[e, which : which + 1, j * LANE : (j + 1) * LANE] = v[e : e + 1]

    @pl.when(g == 0)
    def _():
        last = BLOCKS - 1
        even[1, last * 16 :, LANE:] = jnp.zeros((16, LANE), jnp.bfloat16)
        for side in range(2):
            rest[1, last * 48 :, side * SUB + LANE : (side + 1) * SUB] = jnp.zeros((48, LANE), jnp.bfloat16)
        wa_count = lax.axis_size("wa")
        wa, vert = lax.axis_index("wa"), lax.axis_index("vert")

        def signal(to_wa, to_vert):
            pl.semaphore_signal(
                pltpu.get_barrier_semaphore(), 1, device_id=(to_wa, to_vert), device_id_type=pl.DeviceIdType.MESH
            )

        for i in range(1, vert_count):
            signal(wa, lax.rem(vert + i, vert_count))

        def greet(i, carry):
            to_wa = lax.rem(wa + i, wa_count)
            for to_vert in range(vert_count):
                signal(to_wa, to_vert)
            return carry

        lax.fori_loop(1, wa_count, greet, 0)
        at = lax.broadcasted_iota(jnp.int32, (total, WAVES), 1)
        kind = (at >= CLASS).astype(jnp.int32) + (at >= 2 * CLASS).astype(jnp.int32) + (at >= 3 * CLASS).astype(jnp.int32)
        wave = 4 * (at - CLASS * kind) + kind
        for c in range(per_dest):
            pair = order_ref[:, c // 2 : c // 2 + 1]
            target = TRUNC - pair if c % 2 else pair
            onehot[c * total : (c + 1) * total, :] = (wave == target).astype(jnp.float32).astype(jnp.bfloat16)

    def blocks_of(t):
        return BLOCKS if t == SPAN - 1 else BLOCKS - 1

    def fold(t):
        slot = t % 2
        chunks = min(CHUNKS, 2 * blocks_of(t))
        n = length_ref[t * GROUPS + g] // 4
        for j in range(grid_ref.shape[3] // LANE):
            chunked[slot, j] = grid_ref[t, 0, :, j * LANE : (j + 1) * LANE]
        lane = lax.broadcasted_iota(jnp.int32, (16, LANE), 1)
        quarters = [[chunked[slot, j].astype(jnp.float32) for j in range(chunks)]]
        for part in range(1, 4):
            start = n * part
            whole = start // LANE
            back = LANE - (start - whole * LANE)
            pieces = [chunked[slot, whole + j].astype(jnp.float32) for j in range(chunks + 1)]
            turned = [pltpu.roll(piece, lax.rem(back, LANE), 1) for piece in pieces]
            quarters.append([jnp.where(lane < back, turned[j], turned[j + 1]) for j in range(chunks)])
        for j in range(chunks):
            c1, s1, c2, s2, c3, s3 = (
                twiddle[t * 2 + g % 2, which : which + 1, j * LANE : (j + 1) * LANE] for which in range(6)
            )
            qa, qb, qc, qd = (quarters[part][j] for part in range(4))
            even_sum = qa + qc
            odd_sum = qb + qd
            re = qa - qc
            im = qd - qb
            h2 = even_sum - odd_sum
            q = j // 2
            at = (j % 2) * LANE
            even[slot, q * 16 : q * 16 + 16, at : at + LANE] = jnp.where(
                lane + j * LANE < n, even_sum + odd_sum, 0.0
            ).astype(jnp.bfloat16)
            values = (
                (re * c1 + im * s1, im * c1 - re * s1),
                (h2 * c2, -(h2 * s2)),
                (re * c3 - im * s3, -(im * c3 + re * s3)),
            )
            for r, (zr, zi) in enumerate(values):
                top = (q * 3 + r) * 16
                rest[slot, top : top + 16, at : at + LANE] = zr.astype(jnp.bfloat16)
                rest[slot, top : top + 16, SUB + at : SUB + at + LANE] = zi.astype(jnp.bfloat16)

    def prepare(t):
        fold(t)
        slot = t % 2
        n = jnp.full((8, CPAD), length_ref[t * GROUPS + g] // 4, jnp.int32)
        n_float = n.astype(jnp.float32)
        inv_n = 1.0 / n_float
        u = iota_f((8, CPAD), 1)
        low = iota_f((8, CPAD), 0)
        mixed = jnp.where(low == 0.0, 8.0, jnp.where(low == 1.0, 128.0, 256.0 * (low - 1.0)))
        cb, sb = sincos(turns_of(low * u, n_float, inv_n))
        ct, st = sincos(turns_of(low * 16.0 * u, n_float, inv_n))
        cm, sm = sincos(turns_of(mixed * u, n_float, inv_n))
        small[slot, 0, :8] = ct
        small[slot, 1, :8] = st
        small[slot, 0, 16:] = cm
        small[slot, 1, 16:] = sm
        c8, s8 = small[slot, 0, 16:17, :], small[slot, 1, 16:17, :]
        c128, s128 = small[slot, 0, 17:18, :], small[slot, 1, 17:18, :]
        small[slot, 0, 8:16] = ct * c128 - st * s128
        small[slot, 1, 8:16] = st * c128 + ct * s128
        base = ((cb, sb), (cb * c8 - sb * s8, sb * c8 + cb * s8))
        for a in range(16):
            ca = small[slot, 0, a : a + 1, :]
            sa = small[slot, 1, a : a + 1, :]
            c = jnp.concatenate([x * ca - y * sa for x, y in base], axis=0)
            s = jnp.concatenate([y * ca + x * sa for x, y in base], axis=0)
            c16 = c.astype(jnp.bfloat16)
            s16 = s.astype(jnp.bfloat16)
            rhs[slot, a * 16 : a * 16 + 16, :CPAD] = c16
            rhs[slot, a * 16 : a * 16 + 16, CPAD:] = -s16
            rhs[slot, SUB + a * 16 : SUB + a * 16 + 16, :CPAD] = s16
            rhs[slot, SUB + a * 16 : SUB + a * 16 + 16, CPAD:] = c16

    paired = (g == 1) | (g == 3) | (g == 6)

    def finish(t, sums):
        slot = t % 2
        length = jnp.full((1, CPAD), length_ref[t * GROUPS + g], jnp.int32)
        scale = 1.0 / jnp.sqrt(length.astype(jnp.float32))
        column = lax.broadcasted_iota(jnp.int32, (1, CPAD), 1)
        lane_top = pl.multiple_of(jnp.where(paired, LANE, 0) + t * 32, 32)
        left = [None, None]
        for r in range(4):
            part_sum, first, step = (sums[0], 0, 16) if r == 0 else (sums[1], (r - 1) * 16, 48)
            real = part_sum[first : first + 16, :CPAD]
            imag = part_sum[first : first + 16, CPAD:]
            for q in range(1, blocks_of(t)):
                top = first + q * step
                pr = part_sum[top : top + 16, :CPAD]
                pi = part_sum[top : top + 16, CPAD:]
                c = small[slot, 0, 17 + q : 18 + q, :]
                s = small[slot, 1, 17 + q : 18 + q, :]
                real = real + (pr * c + pi * s)
                imag = imag + (pi * c - pr * s)
            wave = column * 4 + r
            keep = jnp.where((wave * 2 <= length - 1) & (column < CLASS), scale, 0.0)
            for i, value in enumerate((real * keep, imag * keep)):
                if r % 2 == 0:
                    left[i] = value
                    continue
                right = pltpu.roll(value, CPAD - CLASS, 1)
                middle = left[i][:, 2 * LANE :] + right[:, :LANE]
                packed = jnp.concatenate([left[i][:, : 2 * LANE], middle, right[:, LANE:]], axis=1)
                at = (r // 2) * 2 * CLASS
                rows[pl.ds(lane_top + i * 16, 16), at : at + 2 * CLASS] = packed.astype(jnp.bfloat16)

    prepare(0)
    for t in range(SPAN):
        sums = (
            jnp.dot(even[t % 2, : blocks_of(t) * 16], rhs[t % 2, :SUB], preferred_element_type=jnp.float32),
            jnp.dot(rest[t % 2, : blocks_of(t) * 48], rhs[t % 2], preferred_element_type=jnp.float32),
        )
        if t + 1 < SPAN:
            prepare(t + 1)
        finish(t, sums)

    def order(count):
        for c0 in range(0, per_dest, ORDER):
            picked = lax.dot_general(
                onehot[c0 * total : (c0 + ORDER) * total, :],
                rows[: count * LANE, :],
                (((1,), (1,)), ((), ())),
                preferred_element_type=jnp.float32,
            )
            for c in range(ORDER):
                for e in range(count):
                    at = (g - count + 1 + e) * per_dest + c0 + c
                    spread[pl.ds(at, total, stride=dest_rows), :] = picked[
                        c * total : (c + 1) * total, e * LANE : (e + 1) * LANE
                    ]

    pl.when(paired)(lambda: order(2))
    pl.when((g == 4) | (g == 7))(lambda: order(1))

    @pl.when(paired | (g == 4) | (g == 7))
    def _():
        tile = (5 * (g + 1)) // 8 - 1

        def convert(d, carry):
            sending[tile, d] = spread[pl.ds(pl.multiple_of(d * dest_rows + tile * 16, 16), 16), :].astype(jnp.bfloat16)
            return carry

        lax.fori_loop(0, total, convert, 0, unroll=8)

        @pl.when(g == 1)
        def _():
            pl.semaphore_wait(pltpu.get_barrier_semaphore(), total - 1)

        pltpu.make_async_copy(sending.at[tile, me], landing.at[tile, me], local_sem.at[tile]).start()

        wa_count = lax.axis_size("wa")
        wa, vert = lax.axis_index("wa"), lax.axis_index("vert")

        def send(to_wa, to_vert):
            pltpu.make_async_remote_copy(
                sending.at[tile, to_wa * vert_count + to_vert],
                landing.at[tile, me],
                send_sem.at[tile],
                recv_sem.at[tile],
                device_id=(to_wa, to_vert),
                device_id_type=pl.DeviceIdType.MESH,
            ).start()

        for i in range(1, vert_count):
            send(wa, lax.rem(vert + i, vert_count))

        def spoke(i, carry):
            to_wa = lax.rem(wa + i * STRIDE, wa_count)
            for to_vert in range(vert_count):
                send(to_wa, to_vert)
            return carry

        lax.fori_loop(1, wa_count, spoke, 0)

    @pl.when(g == GROUPS - 1)
    def _():
        others = pl.ds(0, total - 1)
        half = lax.axis_size("wa") // 2
        lane = lax.broadcasted_iota(jnp.int32, (16, LANE), 1)
        odd32 = (lane // 32) % 2 == 1
        high64 = lane >= 64

        def regroup(tiles):
            a, b, c, d = tiles
            ab0 = jnp.where(odd32, pltpu.roll(b, 32, 1), a)
            ab1 = jnp.where(odd32, b, pltpu.roll(a, 96, 1))
            cd0 = jnp.where(odd32, pltpu.roll(d, 32, 1), c)
            cd1 = jnp.where(odd32, d, pltpu.roll(c, 96, 1))
            return (
                jnp.where(high64, pltpu.roll(cd0, 64, 1), ab0),
                jnp.where(high64, pltpu.roll(cd1, 64, 1), ab1),
                jnp.where(high64, cd0, pltpu.roll(ab0, 64, 1)),
                jnp.where(high64, cd1, pltpu.roll(ab1, 64, 1)),
            )

        def arrived(tile, carry):
            pltpu.make_async_copy(sending.at[tile, me], landing.at[tile, me], local_sem.at[tile]).wait()
            pltpu.make_async_copy(sending.at[tile, others], landing.at[tile, others], recv_sem.at[tile]).wait()

            def mirror(w, carry):
                north, south = (
                    regroup(
                        [
                            landing[tile, (side * half + w) * vert_count + v].astype(jnp.float32)
                            for v in range(SPAN)
                        ]
                    )
                    for side in range(2)
                )
                for kind in range(2):
                    for t in range(SPAN):
                        value = north[t] - south[t] if kind else north[t] + south[t]
                        top = ((w * 2 + kind) * SPAN + t) * dest_rows + tile * 16
                        spread[pl.ds(pl.multiple_of(top, 16), 16), :] = value
                return carry

            lax.fori_loop(0, half, mirror, 0, unroll=8)
            return carry

        lax.fori_loop(0, landing.shape[0], arrived, 0)

        def gather(w, carry):
            for kind in range(2):
                for t in range(0, SPAN, 2):
                    for col in range(per_dest):
                        both = [
                            spread[
                                pl.ds(((w * 2 + kind) * SPAN + t + e) * dest_rows + col, GROUPS, stride=per_dest), :
                            ]
                            for e in range(2)
                        ]
                        at = ((col % 2) * 2 + kind) * LANE
                        top = pl.multiple_of(w * SPAN * GROUPS + t * GROUPS, 16)
                        out_ref[col // 2, pl.ds(top, 16), at : at + LANE] = jnp.concatenate(both, axis=0).astype(
                            jnp.bfloat16
                        )
            return carry

        lax.fori_loop(0, half, gather, 0, unroll=2)
        for tile in range(landing.shape[0]):
            pltpu.make_async_copy(sending.at[tile, others], landing.at[tile, others], send_sem.at[tile]).wait()


def fourier_all(row_length, pair_order, grid_values, device_total):
    row_total, field_count, points = grid_values.shape
    lat_pairs = row_length.shape[0] * lax.axis_size("wa") // 2
    tiles = WAVES * GROUPS // device_total // 16
    return pl.pallas_call(
        fourier_kernel,
        grid=(GROUPS,),
        in_specs=[
            pl.BlockSpec(memory_space=pltpu.SMEM),
            pl.BlockSpec((device_total, pair_order.shape[0] // device_total), lambda g: (0, 0)),
            pl.BlockSpec((SPAN, 1, field_count, points), lambda g: (0, g, 0, 0)),
        ],
        out_specs=pl.BlockSpec(memory_space=pltpu.VMEM),
        out_shape=jax.ShapeDtypeStruct((WAVES // device_total // 2, lat_pairs, 4 * LANE), jnp.bfloat16),
        scratch_shapes=[
            pltpu.VMEM((2, points // LANE, 16, LANE), jnp.bfloat16),
            pltpu.VMEM((8, 8, CHUNKS * LANE), jnp.float32),
            pltpu.VMEM((2, BLOCKS * 16, SUB), jnp.bfloat16),
            pltpu.VMEM((2, 3 * BLOCKS * 16, 2 * SUB), jnp.bfloat16),
            pltpu.VMEM((2, 2 * SUB, 2 * CPAD), jnp.bfloat16),
            pltpu.VMEM((2, 2, 24, CPAD), jnp.float32),
            pltpu.VMEM((WAVES, WAVES), jnp.bfloat16),
            pltpu.VMEM((2 * LANE, WAVES), jnp.bfloat16),
            pltpu.VMEM((WAVES * GROUPS, LANE), jnp.float32),
            pltpu.VMEM((tiles, device_total, 16, LANE), jnp.bfloat16),
            pltpu.VMEM((tiles, device_total, 16, LANE), jnp.bfloat16),
            pltpu.SemaphoreType.DMA((tiles,)),
            pltpu.SemaphoreType.DMA((tiles,)),
            pltpu.SemaphoreType.DMA((tiles,)),
        ],
        compiler_params=pltpu.CompilerParams(
            vmem_limit_bytes=48 * 2**20, collective_id=0, has_side_effects=True
        ),
        name="fourier",
    )(row_length, pair_order.reshape(device_total, -1), grid_values.reshape(SPAN, GROUPS, field_count, points))


def legendre_kernel(pair_ref, operand, leg_ref, out_ref):
    slot = pl.program_id(0)
    owner = lax.axis_index("wa") * lax.axis_size("vert") + lax.axis_index("vert")
    first_count = WAVES - pair_ref[owner * pl.num_programs(0) + slot]
    columns = leg_ref.shape[1]
    whole = columns // LANE * LANE

    def choose(product, top, out_lanes):
        height = product.shape[0]
        column = lax.broadcasted_iota(jnp.int32, (height, LANE), 0) + top
        in_first = column < first_count
        degree = jnp.where(in_first, column, column - first_count)
        even = degree % 2 == 0
        s0, a0, s1, a1 = (product[:, k * LANE : (k + 1) * LANE] for k in range(4))
        chosen = jnp.where(in_first, jnp.where(even, s0, a0), jnp.where(even, s1, a1))
        turned = chosen.T
        for v in range(4):
            for i in range(2):
                at = v * 32 + i * 16
                out_ref[0, i, v * 16 : v * 16 + 16, out_lanes] = turned[at : at + 16]

    for start in range(0, whole, PART):
        product = jnp.dot(
            leg_ref[slot, start : start + PART, :], operand[slot], preferred_element_type=jnp.float32
        )
        for top in range(0, PART, LANE):
            choose(product[top : top + LANE], start + top, slice(start + top, start + top + LANE))
    last = leg_ref[slot, whole:columns, :]
    product = jnp.dot(
        jnp.broadcast_to(last, (16, last.shape[1])), operand[slot], preferred_element_type=jnp.float32
    )
    column = jnp.zeros((16, LANE), jnp.int32) + whole
    in_first = column < first_count
    degree = jnp.where(in_first, column, column - first_count)
    even = degree % 2 == 0
    s0, a0, s1, a1 = (product[:, k * LANE : (k + 1) * LANE] for k in range(4))
    chosen = jnp.where(in_first, jnp.where(even, s0, a0), jnp.where(even, s1, a1))
    turned = jnp.broadcast_to(chosen[:1], (LANE, LANE)).T
    for v in range(4):
        for i in range(2):
            at = v * 32 + i * 16
            out_ref[0, i, v * 16 : v * 16 + 16, whole:columns] = turned[at : at + 16, : columns - whole]


def legendre_all(operand, legendre, pair_order, vert_count):
    slot_count, lat_pairs, columns = legendre.shape
    field_count = 16 * vert_count
    return pl.pallas_call(
        legendre_kernel,
        grid=(slot_count,),
        in_specs=[
            pl.BlockSpec(memory_space=pltpu.SMEM),
            pl.BlockSpec(memory_space=pltpu.VMEM),
            pl.BlockSpec(memory_space=pltpu.VMEM),
        ],
        out_specs=pl.BlockSpec((1, 2, field_count, columns), lambda s: (s, 0, 0, 0)),
        out_shape=jax.ShapeDtypeStruct((slot_count, 2, field_count, columns), jnp.float32),
        compiler_params=pltpu.CompilerParams(vmem_limit_bytes=24 * 2**20),
        name="legendre",
    )(pair_order, operand, jnp.swapaxes(legendre, 1, 2))


def body(grid_values, row_length, pair_order, legendre):
    wa_count = lax.axis_size("wa")
    vert_count = lax.axis_size("vert")
    device_total = wa_count * vert_count
    operand = fourier_all(row_length, pair_order, grid_values, device_total)
    return legendre_all(operand, legendre, pair_order, vert_count)


def solution(mesh):
    placed = (P("wa", "vert", None), P("wa"), P(), P(("wa", "vert"), None, None))
    return jax.shard_map(
        body,
        mesh=mesh,
        in_specs=placed,
        out_specs=P(("wa", "vert"), None, None, None),
        check_vma=False,
    )
```
